32 devices in a mesh: blk: 16 (over z, x, core), rep: 2 (over y).
Axes of the slice: x: 2, y: 2, z: 4, core: 2. Of those that a mesh axis runs over, the one named last changes fastest.
Arguments:
- features: bfloat16 [16384, 256], P(('blk', 'rep')), may hold values from -6 to 6
- out_grad: bfloat16 [16384, 256], P('blk'), may hold values from -4 to 4
- weight: bfloat16 [256, 256], replicated, may hold values from -0.375 to 0.375
- block_words: int32 [16, 16, 8, 16, 128], P('blk', 'rep'), may hold values from 0 to 255
- block_coords: int32 [16, 16, 2, 8], P('blk', 'rep'), may hold values from 0 to 7, as said below
- block_counts: int32 [16, 16], P('blk', 'rep'), may hold values from 1 to 8, as said below
- degrees: int32 [16384], P('blk'), may hold values from 1 to 127
Outputs:
- input_grad: bfloat16 [16384, 256], P(('blk', 'rep'))
- weight_grad: float32 [256, 256], replicated
The draws below stay inside these ranges and needn't reach their ends.
Inputs may be any that keep to these rules, and one draw needn't show every extreme that they name: `block_coords`: within one slab pair the 8 slots name distinct pairs of row block and column block. `block_counts`: the 8 slab pairs of one device include one in which all 8 slots are live.
All inputs are finite; a program needn't handle non-finite values.
Results may differ from the reference program's by a relative error of at most 0.015.
Values may be sent and summed in bfloat16 or wider, within the bound.
No kernel may reach another device: no remote copies, remote signals or barrier semaphores. Data moves between devices by JAX's collectives and lax.ppermute only.
A program may use at most 64 MiB of HBM per device.

```python
import math
import jax
import jax.numpy as jnp
from jax import lax

F = 256
SLABS = 16
STEPS = 8
RB = 8
BMAX = 8
NODES = 16384


def draw_block_coords(key, part):
    cells = RB * RB
    scores = jax.random.randint(key, (SLABS, SLABS, cells), 0, 65536) * cells + jnp.arange(cells, dtype=jnp.int32)
    order = jnp.argsort(scores, axis=-1)[:, :, :BMAX].astype(jnp.int32)
    return jnp.stack([order // RB, order % RB], axis=2).astype(jnp.int32)


def draw_block_counts(key, part):
    key_one, key_two = jax.random.split(key)
    drawn = jax.random.randint(key_one, (SLABS, SLABS), 0, BMAX)
    counts = 1 + drawn * drawn // BMAX
    groups = SLABS // STEPS
    position = jax.random.randint(key_two, (SLABS, groups), 0, STEPS)
    chosen = jnp.arange(groups, dtype=jnp.int32)[None, :] * STEPS + position
    full_pair = jnp.any(jnp.arange(SLABS, dtype=jnp.int32)[None, None, :] == chosen[:, :, None], axis=1)
    return jnp.where(full_pair, BMAX, counts).astype(jnp.int32)


def draw_degrees(key, part):
    key_one, key_two = jax.random.split(key)
    exponent = jax.random.randint(key_one, (NODES,), 0, 7)
    base = jnp.left_shift(jnp.ones((NODES,), jnp.int32), exponent)
    extra = jax.random.randint(key_two, (NODES,), 0, base)
    return (base + extra).astype(jnp.int32)


def with_ends(entries, rng, low, top_value):
    shape = entries.shape
    index_at = [jax.random.randint(jax.random.fold_in(rng, axis), (), 0, shape[axis]) for axis in range(len(shape))]
    entries = entries.at[tuple(index_at)].set(low)
    longest = shape.index(max(shape))
    index_at[longest] = (index_at[longest] + 1) % shape[longest]
    return entries.at[tuple(index_at)].set(top_value)


def steps_of(key, shape, cuts, least, high):
    factor_of = 1.0
    for dim, parts in cuts:
        heights = jax.random.uniform(jax.random.fold_in(jax.random.fold_in(key, 6), dim), (parts,), jnp.float32, least / len(cuts), high / len(cuts))
        factor_of = factor_of * jnp.repeat(jnp.exp(heights), shape[dim] // parts).reshape((-1,) + (1,) * (len(shape) - 1 - dim))
    return factor_of


def noise(stream_key, dims, spread, reach, cuts=(), kind=jnp.bfloat16):
    loudness = steps_of(stream_key, dims, cuts, -0.22, 0.18) if cuts else 1.0
    values = jax.random.normal(stream_key, dims, jnp.float32) * spread * loudness
    return jnp.minimum(jnp.maximum(values, -reach), reach).astype(kind)


def setup_inputs(seed: int = 0) -> dict:
    keys = jax.random.split(jax.random.key(seed), 8)
    return {
        "features": noise(keys[0], (NODES, F), 1.0, 6.0, ((0, 32),)),
        "out_grad": noise(keys[1], (NODES, F), 0.5, 4.0, ((0, 16),)),
        "weight": noise(keys[2], (F, F), F ** -0.5, 0.375),
        "block_words": with_ends(jax.random.randint(keys[3], (SLABS, SLABS, BMAX, 16, 128), 0, 256), jax.random.fold_in(keys[3], 1), 0, 255).astype(jnp.int32),
        "block_coords": draw_block_coords(jax.random.fold_in(keys[7], 71), 0),
        "block_counts": draw_block_counts(jax.random.fold_in(keys[7], 71), 0),
        "degrees": draw_degrees(jax.random.fold_in(keys[7], 71), 0),
    }


def unpack_block(slot_words):
    shifts = jnp.arange(8, dtype=jnp.int32)
    bit_values = jnp.bitwise_and(jnp.right_shift(slot_words[:, :, None, :], shifts[None, None, :, None]), 1)
    return bit_values.reshape(slot_words.shape[0], 128, 128).astype(jnp.float32)

def reference(features, out_grad, weight, block_words, block_coords, block_counts, degrees):
    inverse_root = lax.rsqrt(degrees.astype(jnp.float32))
    scaled = (out_grad.astype(jnp.float32) * inverse_root[:, None]).astype(jnp.bfloat16)
    slabs = scaled.reshape(SLABS, RB, 128, F)
    column_ids = jnp.arange(RB, dtype=jnp.int32)
    slot_ids = jnp.arange(BMAX, dtype=jnp.int32)

    def one_target(target):

        def one_pair(accumulated, offset):
            source = (target + offset) % SLABS
            coords = block_coords[target, offset]
            live_count = block_counts[target, offset]
            picked = jnp.take(slabs[source], coords[0], axis=0).astype(jnp.float32)
            transposed = unpack_block(block_words[target, offset])
            contrib = jnp.einsum('bvu,buf->bvf', transposed, picked)
            live_slots = slot_ids < live_count
            placement = ((coords[1][:, None] == column_ids[None, :]) & live_slots[:, None]).astype(jnp.float32)
            return (accumulated + jnp.einsum('bc,bvf->cvf', placement, contrib), None)
        accumulated, _ = lax.scan(one_pair, jnp.zeros((RB, 128, F), jnp.float32), jnp.arange(SLABS, dtype=jnp.int32))
        return accumulated
    summed = lax.map(one_target, jnp.arange(SLABS, dtype=jnp.int32)).reshape(NODES, F)
    aggregated = (summed * inverse_root[:, None]).astype(jnp.bfloat16)
    input_grad = jnp.dot(aggregated, weight.T, preferred_element_type=jnp.float32).astype(jnp.bfloat16)
    weight_grad = jnp.dot(features.T, aggregated, preferred_element_type=jnp.float32) * (1.0 / math.sqrt(NODES))
    return (input_grad, weight_grad)
```

```python
import functools
import math

import jax
import jax.numpy as jnp
from jax import lax
from jax.experimental import pallas as pl
from jax.experimental.pallas import tpu as pltpu
from jax.sharding import PartitionSpec as P

CORES = 2
COLUMNS = 2


def device_of(row, column, core):
    return (row * COLUMNS + column) * CORES + core


def places(blk_size):
    rows = blk_size // (COLUMNS * CORES)
    return [(z, x, c) for z in range(rows) for x in range(COLUMNS) for c in range(CORES)]


def ring_order(rows):
    return [(z, 0) for z in range(rows)] + [(z, 1) for z in reversed(range(rows))]


def along_ring(block, distance):
    rows = lax.axis_size("blk") // (COLUMNS * CORES)
    order = ring_order(rows)
    route = []
    for place, (z, x) in enumerate(order):
        to_z, to_x = order[(place + distance) % len(order)]
        route += [(device_of(z, x, c), device_of(to_z, to_x, c)) for c in range(CORES)]
    return lax.ppermute(block, "blk", route)


def along_rows(block, distance):
    rows = lax.axis_size("blk") // (COLUMNS * CORES)
    route = [
        (device_of(z, x, c), device_of((z + distance) % rows, x, c))
        for z, x, c in places(lax.axis_size("blk"))
    ]
    return lax.ppermute(block, "blk", route)


def across_columns(block):
    route = [
        (device_of(z, x, c), device_of(z, 1 - x, c)) for z, x, c in places(lax.axis_size("blk"))
    ]
    return lax.ppermute(block, "blk", route)


def across_cores(block):
    route = [
        (device_of(z, x, c), device_of(z, x, 1 - c)) for z, x, c in places(lax.axis_size("blk"))
    ]
    return lax.ppermute(block, "blk", route)


def along_rep(block, distance):
    size = lax.axis_size("rep")
    return lax.ppermute(block, "rep", [(i, (i + distance) % size) for i in range(size)])


def from_all_reps(block):
    return [block] + [along_rep(block, d) for d in range(1, lax.axis_size("rep"))]


def tree_sum(terms):
    while len(terms) > 1:
        half = len(terms) // 2
        terms = [terms[d] + terms[d + half] for d in range(half)]
    return terms[0]


def add_pairs(index_ref, facts, words, slabs, sums_ref, slot_total):
    bit_ids = lax.broadcasted_iota(jnp.int32, (16, 8, 128), 1)
    fact_width = 1 + 2 * slot_total
    for slab_id, slab_ref in enumerate(slabs):
        for target in range(2):
            pair = index_ref[slab_id * 2 + target]
            base = pair * fact_width
            live_count = facts[target][base]
            for slot in range(slot_total):
                row_block = facts[target][base + 1 + slot]
                column_block = facts[target][base + 1 + slot_total + slot]
                live = jnp.where(slot < live_count, 255, 0)
                slot_words = jnp.bitwise_and(words[target][pair, slot].astype(jnp.int32), live)
                bits = jnp.bitwise_and(jnp.right_shift(slot_words[:, None, :], bit_ids), 1)
                transposed = bits.reshape(128, 128).astype(jnp.float32).astype(jnp.bfloat16)
                rows = pl.ds(pl.multiple_of(row_block * 128, 128), 128)
                columns = pl.ds(pl.multiple_of(column_block * 128, 128), 128)
                sums_ref[target, columns, :] += jnp.dot(
                    transposed, slab_ref[rows, :], preferred_element_type=jnp.float32
                )


def step_kernel(slab_total, slot_total, first, index_ref, fact_a, fact_b, words_a, words_b, *refs):
    slabs = refs[:slab_total]
    sums_ref = refs[-1]
    if first:
        sums_ref[...] = jnp.zeros_like(sums_ref)
    else:
        sums_ref[...] = refs[slab_total][...]
    add_pairs(index_ref, (fact_a, fact_b), (words_a, words_b), slabs, sums_ref, slot_total)


def last_kernel(
    slot_total, rep_size, index_ref, order_ref, fact_a, fact_b, words_a, words_b, slab_ref, sums_in,
    features_ref, roots_ref, own_ref, other_ref, term_ref, sums_ref,
):
    sums_ref[...] = sums_in[...]
    add_pairs(index_ref, (fact_a, fact_b), (words_a, words_b), [slab_ref], sums_ref, slot_total)
    own_ref[...] = sums_ref[0]
    other_ref[...] = sums_ref[1]
    share = sums_ref.shape[1] // rep_size
    term = jnp.zeros(term_ref.shape, jnp.float32)
    for target in range(2):
        for d in range(rep_size):
            rows = pl.ds(pl.multiple_of(order_ref[d] * share, share), share)
            part = (sums_ref[target, rows, :] * roots_ref[target, rows, :]).astype(jnp.bfloat16)
            term += jnp.dot(features_ref[d, target], part, preferred_element_type=jnp.float32)
    term_ref[...] = term.astype(term_ref.dtype)


SMEM = pl.BlockSpec(memory_space=pltpu.SMEM)
VMEM = pl.BlockSpec(memory_space=pltpu.VMEM)
PARAMS = pltpu.CompilerParams(vmem_limit_bytes=48 * 1024 * 1024)


def per_device(features, out_grad, weight, block_words, block_coords, block_counts, degrees):
    slab_rows, width = out_grad.shape
    rep_size = lax.axis_size("rep")
    blk_size = lax.axis_size("blk")
    chips = blk_size // CORES
    rows_of_chips = chips // COLUMNS
    rep_index = lax.axis_index("rep")
    blk_index = lax.axis_index("blk")
    core = blk_index % CORES
    chip = blk_index // CORES
    share_width = width // rep_size
    share_rows = slab_rows // rep_size
    slot_total = block_words.shape[2]
    half_steps = block_words.shape[1] // 2

    inverse_root = lax.rsqrt(degrees.astype(jnp.float32))
    own_columns = lax.dynamic_slice_in_dim(out_grad, rep_index * share_width, share_width, 1)
    scaled = (own_columns.astype(jnp.float32) * inverse_root[:, None]).astype(jnp.bfloat16)

    words = block_words[0].astype(jnp.int16).reshape(half_steps, 2, slot_total, 16, 128)
    facts = jnp.concatenate(
        [block_counts[0][:, None], block_coords[0].reshape(2 * half_steps, 2 * slot_total)], axis=1
    ).reshape(half_steps, 2, 1 + 2 * slot_total)
    words = jnp.stack([words[:, 0], across_cores(words[:, 1])])
    facts = jnp.stack([facts[:, 0], across_cores(facts[:, 1])])
    words = jnp.concatenate(from_all_reps(words), axis=1)
    facts = jnp.concatenate(from_all_reps(facts), axis=1)
    words_a, words_b = words[0], words[1]
    fact_a, fact_b = facts[0].reshape(-1), facts[1].reshape(-1)

    turned = features.T
    turned = jnp.stack([turned, across_cores(turned)])
    turned = jnp.stack(from_all_reps(turned))
    roots = jnp.stack([inverse_root, across_cores(inverse_root)])
    roots = jnp.broadcast_to(roots[:, :, None], (2, slab_rows, share_width))

    ring_row = chip // COLUMNS
    place = jnp.where(chip % COLUMNS == 0, ring_row, chips - 1 - ring_row)

    def pair_indices(distances):
        entries = []
        for distance in distances:
            at = (place + distance) % chips
            source = jnp.where(
                at < rows_of_chips, at * COLUMNS, (chips - 1 - at) * COLUMNS + 1
            )
            for target in range(2):
                offset = (source - chip - jnp.where(core == 0, target, 0)) % chips
                behind = (rep_index - offset // half_steps) % rep_size
                entries.append(behind * half_steps + offset % half_steps)
        return jnp.stack(entries).astype(jnp.int32)

    pair_cost = 2 * slot_total * 128 * 128 * share_width * 2
    sums_shape = jax.ShapeDtypeStruct((2, slab_rows, share_width), jnp.float32)

    def add_step(distances, slabs, sums):
        first = sums is None
        operands = [pair_indices(distances), fact_a, fact_b, words_a, words_b, *slabs]
        specs = [SMEM] * 3 + [VMEM] * (2 + len(slabs))
        aliases = {}
        if not first:
            aliases = {len(operands): 0}
            operands.append(sums)
            specs.append(VMEM)
        return pl.pallas_call(
            functools.partial(step_kernel, len(slabs), slot_total, first),
            out_shape=sums_shape,
            in_specs=specs,
            out_specs=VMEM,
            input_output_aliases=aliases,
            compiler_params=PARAMS,
            cost_estimate=pl.CostEstimate(
                flops=pair_cost * len(slabs), bytes_accessed=4 << 20, transcendentals=0
            ),
            name="add_step",
        )(*operands)

    sums = add_step([0], [scaled], None)
    forward = backward = scaled
    for step in range(1, chips // 2):
        forward, backward = along_ring(forward, 1), along_ring(backward, -1)
        sums = add_step([-step, step], [forward, backward], sums)
    forward = along_ring(forward, 1)

    order = ((rep_index - jnp.arange(rep_size, dtype=jnp.int32)) % rep_size).astype(jnp.int32)
    slab_shape = jax.ShapeDtypeStruct((slab_rows, share_width), jnp.float32)
    own_sums, other_sums, term = pl.pallas_call(
        functools.partial(last_kernel, slot_total, rep_size),
        out_shape=(slab_shape, slab_shape, jax.ShapeDtypeStruct((width, share_width), jnp.bfloat16)),
        in_specs=[SMEM] * 4 + [VMEM] * 6,
        out_specs=(VMEM,) * 3,
        scratch_shapes=[pltpu.VMEM(sums_shape.shape, jnp.float32)],
        compiler_params=PARAMS,
        name="last_step",
    )(
        pair_indices([chips // 2]), order, fact_a, fact_b, words_a, words_b, forward, sums,
        turned, roots,
    )

    total = tree_sum(
        [t.astype(jnp.float32) for t in [term] + [along_rows(term, d) for d in range(1, rows_of_chips)]]
    ).astype(jnp.bfloat16)
    total = total.astype(jnp.float32) + across_columns(total).astype(jnp.float32)
    total = total + across_cores(total)
    total = total * (1.0 / math.sqrt(slab_rows * blk_size))
    weight_grad = jnp.zeros((width, width), jnp.float32)
    for d, columns in enumerate(from_all_reps(total)):
        at = ((rep_index - d) % rep_size) * share_width
        weight_grad = lax.dynamic_update_slice_in_dim(weight_grad, columns, at, 1)

    own_sums = own_sums + across_cores(other_sums)
    aggregated = (own_sums * inverse_root[:, None]).astype(jnp.bfloat16)
    result = jnp.zeros((share_rows, width), jnp.float32)
    for d in range(rep_size):
        rows_to = ((rep_index + d) % rep_size) * share_rows
        part = lax.dynamic_slice_in_dim(aggregated, rows_to, share_rows, 0)
        if d:
            part = along_rep(part, d)
        columns_at = ((rep_index - d) % rep_size) * share_width
        side = lax.dynamic_slice_in_dim(weight, columns_at, share_width, 1)
        result = result + lax.dot_general(
            part, side, (((1,), (1,)), ((), ())), preferred_element_type=jnp.float32
        )
    return (result.astype(jnp.bfloat16), weight_grad)


def solution(mesh):
    return jax.shard_map(
        per_device,
        mesh=mesh,
        in_specs=(
            P(("blk", "rep"), None),
            P("blk", None),
            P(),
            P("blk", "rep", None, None, None),
            P("blk", "rep", None, None),
            P("blk", "rep"),
            P("blk"),
        ),
        out_specs=(P(("blk", "rep"), None), P()),
        check_vma=False,
    )
```

```python
import functools
import math

import jax
import jax.numpy as jnp
from jax import lax
from jax.experimental import pallas as pl
from jax.experimental.pallas import tpu as pltpu
from jax.sharding import PartitionSpec as P

CORES = 2
COLUMNS = 2


def device_of(row, column, core):
    return (row * COLUMNS + column) * CORES + core


def places(blk_size):
    rows = blk_size // (COLUMNS * CORES)
    return [(z, x, c) for z in range(rows) for x in range(COLUMNS) for c in range(CORES)]


def ring_order(rows):
    return [(z, 0) for z in range(rows)] + [(z, 1) for z in reversed(range(rows))]


def along_ring(block, distance):
    rows = lax.axis_size("blk") // (COLUMNS * CORES)
    order = ring_order(rows)
    route = []
    for place, (z, x) in enumerate(order):
        to_z, to_x = order[(place + distance) % len(order)]
        route += [(device_of(z, x, c), device_of(to_z, to_x, c)) for c in range(CORES)]
    return lax.ppermute(block, "blk", route)


def across_rows(block, distance):
    route = [
        (device_of(z, x, c), device_of(z ^ distance, x, c))
        for z, x, c in places(lax.axis_size("blk"))
    ]
    return lax.ppermute(block, "blk", route)


def across_columns(block):
    route = [
        (device_of(z, x, c), device_of(z, 1 - x, c)) for z, x, c in places(lax.axis_size("blk"))
    ]
    return lax.ppermute(block, "blk", route)


def across_cores(block):
    route = [
        (device_of(z, x, c), device_of(z, x, 1 - c)) for z, x, c in places(lax.axis_size("blk"))
    ]
    return lax.ppermute(block, "blk", route)


def along_rep(block, distance):
    size = lax.axis_size("rep")
    return lax.ppermute(block, "rep", [(i, (i + distance) % size) for i in range(size)])


def across_columns_and_rep(block, distance):
    size = lax.axis_size("rep")
    route = [
        (device_of(z, x, c) * size + r, device_of(z, 1 - x, c) * size + (r + distance) % size)
        for z, x, c in places(lax.axis_size("blk"))
        for r in range(size)
    ]
    return lax.ppermute(block, ("blk", "rep"), route)


def from_all_reps(block):
    return [block] + [along_rep(block, d) for d in range(1, lax.axis_size("rep"))]


def add_pairs(index_ref, facts, words, slabs, sums_ref, slot_total):
    bit_ids = lax.broadcasted_iota(jnp.int32, (16, 8, 128), 1)
    fact_width = 1 + 2 * slot_total
    for slab_id, slab_ref in enumerate(slabs):
        for target in range(2):
            pair = index_ref[slab_id * 2 + target]
            base = pair * fact_width
            live_count = facts[target][base]
            for slot in range(slot_total):
                row_block = facts[target][base + 1 + slot]
                column_block = facts[target][base + 1 + slot_total + slot]
                live = jnp.where(slot < live_count, 255, 0)
                slot_words = words[target][pair, slot * 16 : slot * 16 + 16, :].astype(jnp.int32)
                slot_words = jnp.bitwise_and(slot_words, live)
                bits = jnp.bitwise_and(jnp.right_shift(slot_words[:, None, :], bit_ids), 1)
                transposed = bits.reshape(128, 128).astype(jnp.float32).astype(jnp.bfloat16)
                rows = pl.ds(pl.multiple_of(row_block * 128, 128), 128)
                columns = pl.ds(pl.multiple_of(column_block * 128, 128), 128)
                sums_ref[target, columns, :] += jnp.dot(
                    transposed, slab_ref[rows, :], preferred_element_type=jnp.float32
                )


def fill(slab_buffer, halves):
    half = slab_buffer.shape[1] // 2
    for slab_id in range(len(halves) // 2):
        slab_buffer[slab_id, :half, :] = halves[2 * slab_id][...]
        slab_buffer[slab_id, half:, :] = halves[2 * slab_id + 1][...]
    return [slab_buffer.at[slab_id] for slab_id in range(len(halves) // 2)]


def step_kernel(half_total, slot_total, first, index_ref, fact_a, fact_b, words_a, words_b, *refs):
    halves, sums_ref, slab_buffer = refs[:half_total], refs[-2], refs[-1]
    if first:
        sums_ref[...] = jnp.zeros_like(sums_ref)
    else:
        sums_ref[...] = refs[half_total][...]
    slabs = fill(slab_buffer, halves)
    add_pairs(index_ref, (fact_a, fact_b), (words_a, words_b), slabs, sums_ref, slot_total)


def last_kernel(
    slot_total, rep_size, index_ref, order_ref, fact_a, fact_b, words_a, words_b, low_ref, high_ref,
    sums_in, own_features, other_features, own_ref, other_ref, keep_ref, send_ref,
    sums_ref, term_ref, slab_buffer,
):
    sums_ref[...] = sums_in[...]
    slabs = fill(slab_buffer, [low_ref, high_ref])
    add_pairs(index_ref, (fact_a, fact_b), (words_a, words_b), slabs, sums_ref, slot_total)
    own_ref[...] = sums_ref[0]
    other_ref[...] = sums_ref[1]
    share = sums_ref.shape[1] // rep_size
    term = jnp.zeros(term_ref.shape, jnp.float32)
    for target, features_ref in enumerate((own_features, other_features)):
        for d in range(rep_size):
            rows = pl.ds(pl.multiple_of(order_ref[d] * share, share), share)
            part = sums_ref[target, rows, :].astype(jnp.bfloat16)
            term += jnp.dot(features_ref[d], part, preferred_element_type=jnp.float32)
    term_ref[...] = term
    half = term_ref.shape[0] // 2
    core = order_ref[rep_size]
    keep_ref[...] = term_ref[pl.ds(pl.multiple_of(core * half, half), half), :]
    send_ref[...] = term_ref[pl.ds(pl.multiple_of((1 - core) * half, half), half), :]


SMEM = pl.BlockSpec(memory_space=pltpu.SMEM)
VMEM = pl.BlockSpec(memory_space=pltpu.VMEM)
PARAMS = pltpu.CompilerParams(vmem_limit_bytes=48 * 1024 * 1024)


def per_device(features, out_grad, weight, block_words, block_coords, block_counts, degrees):
    slab_rows, width = out_grad.shape
    rep_size = lax.axis_size("rep")
    blk_size = lax.axis_size("blk")
    chips = blk_size // CORES
    rows_of_chips = chips // COLUMNS
    rep_index = lax.axis_index("rep")
    blk_index = lax.axis_index("blk")
    core = blk_index % CORES
    chip = blk_index // CORES
    share_width = width // rep_size
    share_rows = slab_rows // rep_size
    slot_total = block_words.shape[2]
    half_steps = block_words.shape[1] // 2

    inverse_root = lax.rsqrt(degrees.astype(jnp.float32))
    own_columns = lax.dynamic_slice_in_dim(out_grad, rep_index * share_width, share_width, 1)
    scaled = (own_columns.astype(jnp.float32) * inverse_root[:, None]).astype(jnp.bfloat16)

    step_total = 2 * half_steps
    facts = jnp.concatenate(
        [block_counts[0][:, None], block_coords[0].reshape(step_total, 2 * slot_total)], axis=1
    )
    facts = jnp.pad(facts, ((0, 0), (0, 2048 - facts.shape[1]))).reshape(step_total, 16, 128)
    words = jnp.concatenate([block_words[0].reshape(step_total, slot_total * 16, 128), facts], axis=1)
    words = jnp.stack(from_all_reps(words.astype(jnp.int16)))
    words = words.reshape(rep_size, half_steps, 2, slot_total * 16 + 16, 128)
    words_a = words[:, :, 0].reshape(rep_size * half_steps, slot_total * 16 + 16, 128)
    words_b = across_cores(words[:, :, 1].reshape(rep_size * half_steps, slot_total * 16 + 16, 128))

    def facts_of(words):
        facts = words[:, slot_total * 16 :].reshape(-1, 2048)[:, : 1 + 2 * slot_total]
        return facts.astype(jnp.int32).reshape(-1)

    fact_a, fact_b = facts_of(words_a), facts_of(words_b)

    share_root = lax.dynamic_slice_in_dim(inverse_root, rep_index * share_rows, share_rows, 0)
    turned = (features.T.astype(jnp.float32) * share_root[None, :]).astype(jnp.bfloat16)
    own_features = jnp.stack(from_all_reps(turned))
    other_features = across_cores(own_features)

    ring_row = chip // COLUMNS
    place = jnp.where(chip % COLUMNS == 0, ring_row, chips - 1 - ring_row)

    def pair_indices(distances):
        entries = []
        for distance in distances:
            at = (place + distance) % chips
            source = jnp.where(
                at < rows_of_chips, at * COLUMNS, (chips - 1 - at) * COLUMNS + 1
            )
            for target in range(2):
                offset = (source - chip - jnp.where(core == 0, target, 0)) % chips
                behind = (rep_index - offset // half_steps) % rep_size
                entries.append(behind * half_steps + offset % half_steps)
        return jnp.stack(entries).astype(jnp.int32)

    pair_cost = 2 * slot_total * 128 * 128 * share_width * 2
    sums_shape = jax.ShapeDtypeStruct((2, slab_rows, share_width), jnp.float32)

    def add_step(distances, halves, sums):
        first = sums is None
        operands = [pair_indices(distances), fact_a, fact_b, words_a, words_b, *halves]
        specs = [SMEM] * 3 + [VMEM] * (2 + len(halves))
        aliases = {}
        if not first:
            aliases = {len(operands): 0}
            operands.append(sums)
            specs.append(VMEM)
        slab_total = len(halves) // 2
        return pl.pallas_call(
            functools.partial(step_kernel, len(halves), slot_total, first),
            out_shape=sums_shape,
            in_specs=specs,
            out_specs=VMEM,
            input_output_aliases=aliases,
            scratch_shapes=[pltpu.VMEM((slab_total, slab_rows, share_width), jnp.bfloat16)],
            compiler_params=PARAMS,
            cost_estimate=pl.CostEstimate(
                flops=pair_cost * slab_total, bytes_accessed=4 << 20, transcendentals=0
            ),
            name="add_step",
        )(*operands)

    low, high = scaled[: slab_rows // 2], scaled[slab_rows // 2 :]
    sums = add_step([0], [low, high], None)
    low_up = low_down = low
    high_up = high_down = high
    for step in range(1, chips // 2):
        low_up, high_down = along_ring(low_up, 1), along_ring(high_down, -1)
        high_up, low_down = along_ring(high_up, 1), along_ring(low_down, -1)
        sums = add_step([-step, step], [low_up, high_up, low_down, high_down], sums)
    low_up, high_down = along_ring(low_up, 1), along_ring(high_down, -1)

    order = (rep_index - jnp.arange(rep_size, dtype=jnp.int32)) % rep_size
    order = jnp.concatenate([order, core[None]]).astype(jnp.int32)
    slab_shape = jax.ShapeDtypeStruct((slab_rows, share_width), jnp.float32)
    half_term = jax.ShapeDtypeStruct((width // 2, share_width), jnp.float32)
    own_sums, other_sums, keep, send = pl.pallas_call(
        functools.partial(last_kernel, slot_total, rep_size),
        out_shape=(slab_shape, slab_shape, half_term, half_term),
        in_specs=[SMEM] * 4 + [VMEM] * 7,
        out_specs=(VMEM,) * 4,
        scratch_shapes=[
            pltpu.VMEM(sums_shape.shape, jnp.float32),
            pltpu.VMEM((width, share_width), jnp.float32),
            pltpu.VMEM((1, slab_rows, share_width), jnp.bfloat16),
        ],
        compiler_params=PARAMS,
        name="last_step",
    )(
        pair_indices([chips // 2]), order, fact_a, fact_b, words_a, words_b, low_up, high_down, sums,
        own_features, other_features,
    )

    total = keep + across_cores(send)
    distance = 1
    while distance < rows_of_chips:
        total = total.astype(jnp.bfloat16)
        total = total.astype(jnp.float32) + across_rows(total, distance).astype(jnp.float32)
        distance *= 2
    total = total.astype(jnp.bfloat16)
    weight_half = jnp.zeros((width // 2, width), jnp.float32)
    for d in range(rep_size):
        near, far = total, across_columns(total)
        if d:
            near, far = along_rep(total, d), across_columns_and_rep(total, d)
        columns = near.astype(jnp.float32) + far.astype(jnp.float32)
        at = ((rep_index - d) % rep_size) * share_width
        weight_half = lax.dynamic_update_slice_in_dim(weight_half, columns, at, 1)
    weight_half = weight_half * (1.0 / math.sqrt(slab_rows * blk_size))
    other_half = across_cores(weight_half)
    weight_grad = jnp.concatenate(
        [jnp.where(core == 0, weight_half, other_half), jnp.where(core == 0, other_half, weight_half)]
    )

    own_sums = own_sums + across_cores(other_sums)
    aggregated = (own_sums * inverse_root[:, None]).astype(jnp.bfloat16)
    result = jnp.zeros((share_rows, width), jnp.float32)
    for d in range(rep_size):
        rows_to = ((rep_index + d) % rep_size) * share_rows
        part = lax.dynamic_slice_in_dim(aggregated, rows_to, share_rows, 0)
        if d:
            part = along_rep(part, d)
        columns_at = ((rep_index - d) % rep_size) * share_width
        side = lax.dynamic_slice_in_dim(weight, columns_at, share_width, 1)
        result = result + lax.dot_general(
            part, side, (((1,), (1,)), ((), ())), preferred_element_type=jnp.float32
        )
    return (result.astype(jnp.bfloat16), weight_grad)


def solution(mesh):
    return jax.shard_map(
        per_device,
        mesh=mesh,
        in_specs=(
            P(("blk", "rep"), None),
            P("blk", None),
            P(),
            P("blk", "rep", None, None, None),
            P("blk", "rep", None, None),
            P("blk", "rep"),
            P("blk"),
        ),
        out_specs=(P(("blk", "rep"), None), P()),
        check_vma=False,
    )
```

```python
import functools
import math

import jax
import jax.numpy as jnp
from jax import lax
from jax.experimental import pallas as pl
from jax.experimental.pallas import tpu as pltpu
from jax.sharding import PartitionSpec as P

CORES = 2
COLUMNS = 2


def device_of(row, column, core):
    return (row * COLUMNS + column) * CORES + core


def places(blk_size):
    rows = blk_size // (COLUMNS * CORES)
    return [(z, x, c) for z in range(rows) for x in range(COLUMNS) for c in range(CORES)]


def ring_order(rows):
    return [(z, 0) for z in range(rows)] + [(z, 1) for z in reversed(range(rows))]


def along_ring(block, distance):
    rows = lax.axis_size("blk") // (COLUMNS * CORES)
    order = ring_order(rows)
    route = []
    for place, (z, x) in enumerate(order):
        to_z, to_x = order[(place + distance) % len(order)]
        route += [(device_of(z, x, c), device_of(to_z, to_x, c)) for c in range(CORES)]
    return lax.ppermute(block, "blk", route)


def across_rows(block, distance):
    route = [
        (device_of(z, x, c), device_of(z ^ distance, x, c))
        for z, x, c in places(lax.axis_size("blk"))
    ]
    return lax.ppermute(block, "blk", route)


def across_columns(block):
    route = [
        (device_of(z, x, c), device_of(z, 1 - x, c)) for z, x, c in places(lax.axis_size("blk"))
    ]
    return lax.ppermute(block, "blk", route)


def across_cores(block):
    route = [
        (device_of(z, x, c), device_of(z, x, 1 - c)) for z, x, c in places(lax.axis_size("blk"))
    ]
    return lax.ppermute(block, "blk", route)


def along_rep(block, distance):
    size = lax.axis_size("rep")
    return lax.ppermute(block, "rep", [(i, (i + distance) % size) for i in range(size)])


def along_rep(block, distance):
    size = lax.axis_size("rep")
    return lax.ppermute(block, "rep", [(i, (i + distance) % size) for i in range(size)])


def across_columns_and_rep(block, distance):
    size = lax.axis_size("rep")
    route = [
        (device_of(z, x, c) * size + r, device_of(z, 1 - x, c) * size + (r + distance) % size)
        for z, x, c in places(lax.axis_size("blk"))
        for r in range(size)
    ]
    return lax.ppermute(block, ("blk", "rep"), route)


def from_all_reps(block):
    return [block] + [along_rep(block, d) for d in range(1, lax.axis_size("rep"))]


def add_pairs(index_ref, facts, words, slabs, sums_ref, slot_total):
    bit_ids = lax.broadcasted_iota(jnp.int32, (16, 8, 128), 1)
    fact_width = 1 + 2 * slot_total
    for slab_id, slab_ref in enumerate(slabs):
        for target in range(2):
            pair = index_ref[slab_id * 2 + target]
            base = pair * fact_width
            live_count = facts[target][base]
            for slot in range(slot_total):
                row_block = facts[target][base + 1 + slot]
                column_block = facts[target][base + 1 + slot_total + slot]
                live = jnp.where(slot < live_count, 255, 0)
                slot_words = words[target][pair, slot * 16 : slot * 16 + 16, :].astype(jnp.int32)
                slot_words = jnp.bitwise_and(slot_words, live)
                bits = jnp.bitwise_and(jnp.right_shift(slot_words[:, None, :], bit_ids), 1)
                transposed = bits.reshape(128, 128).astype(jnp.float32).astype(jnp.bfloat16)
                rows = pl.ds(pl.multiple_of(row_block * 128, 128), 128)
                columns = pl.ds(pl.multiple_of(column_block * 128, 128), 128)
                sums_ref[target, columns, :] += jnp.dot(
                    transposed, slab_ref[rows, :], preferred_element_type=jnp.float32
                )


def step_kernel(slab_total, slot_total, first, index_ref, fact_a, fact_b, words_a, words_b, *refs):
    slabs, sums_ref = refs[:slab_total], refs[-1]
    if first:
        sums_ref[...] = jnp.zeros_like(sums_ref)
    else:
        sums_ref[...] = refs[slab_total][...]
    add_pairs(index_ref, (fact_a, fact_b), (words_a, words_b), slabs, sums_ref, slot_total)


def last_kernel(
    slot_total, rep_size, index_ref, order_ref, fact_a, fact_b, words_a, words_b, slab_ref,
    sums_in, own_features, other_features, own_ref, other_ref, keep_ref, send_ref,
    sums_ref, term_ref,
):
    sums_ref[...] = sums_in[...]
    add_pairs(index_ref, (fact_a, fact_b), (words_a, words_b), [slab_ref], sums_ref, slot_total)
    own_ref[...] = sums_ref[0]
    other_ref[...] = sums_ref[1]
    share = sums_ref.shape[1] // rep_size
    term = jnp.zeros(term_ref.shape, jnp.float32)
    for target, features_ref in enumerate((own_features, other_features)):
        for d in range(rep_size):
            rows = pl.ds(pl.multiple_of(order_ref[d] * share, share), share)
            part = sums_ref[target, rows, :].astype(jnp.bfloat16)
            term += jnp.dot(features_ref[d], part, preferred_element_type=jnp.float32)
    term_ref[...] = term
    half = term_ref.shape[0] // 2
    core = order_ref[rep_size]
    keep_ref[...] = term_ref[pl.ds(pl.multiple_of(core * half, half), half), :]
    send_ref[...] = term_ref[pl.ds(pl.multiple_of((1 - core) * half, half), half), :]


SMEM = pl.BlockSpec(memory_space=pltpu.SMEM)
VMEM = pl.BlockSpec(memory_space=pltpu.VMEM)
PARAMS = pltpu.CompilerParams(vmem_limit_bytes=24 * 1024 * 1024)


def per_device(features, out_grad, weight, block_words, block_coords, block_counts, degrees):
    slab_rows, width = out_grad.shape
    rep_size = lax.axis_size("rep")
    blk_size = lax.axis_size("blk")
    chips = blk_size // CORES
    rows_of_chips = chips // COLUMNS
    rep_index = lax.axis_index("rep")
    blk_index = lax.axis_index("blk")
    core = blk_index % CORES
    chip = blk_index // CORES
    share_width = width // rep_size
    share_rows = slab_rows // rep_size
    slot_total = block_words.shape[2]
    half_steps = block_words.shape[1] // 2

    inverse_root = lax.rsqrt(degrees.astype(jnp.float32))
    own_columns = lax.dynamic_slice_in_dim(out_grad, rep_index * share_width, share_width, 1)
    scaled = (own_columns.astype(jnp.float32) * inverse_root[:, None]).astype(jnp.bfloat16)

    forward, backward = along_ring(scaled, 1), along_ring(scaled, -1)

    step_total = 2 * half_steps
    facts = jnp.concatenate(
        [block_counts[0][:, None], block_coords[0].reshape(step_total, 2 * slot_total)], axis=1
    )
    facts = jnp.pad(facts, ((0, 0), (0, 2048 - facts.shape[1]))).reshape(step_total, 16, 128)
    words = jnp.concatenate([block_words[0].reshape(step_total, slot_total * 16, 128), facts], axis=1)
    words = jnp.stack(from_all_reps(words.astype(jnp.int16)))
    words = words.reshape(rep_size, half_steps, 2, slot_total * 16 + 16, 128)
    words_a = words[:, :, 0].reshape(rep_size * half_steps, slot_total * 16 + 16, 128)
    words_b = across_cores(words[:, :, 1].reshape(rep_size * half_steps, slot_total * 16 + 16, 128))

    def facts_of(words):
        facts = words[:, slot_total * 16 :].reshape(-1, 2048)[:, : 1 + 2 * slot_total]
        return facts.astype(jnp.int32).reshape(-1)

    fact_a, fact_b = facts_of(words_a), facts_of(words_b)

    share_root = lax.dynamic_slice_in_dim(inverse_root, rep_index * share_rows, share_rows, 0)
    turned = (features.T.astype(jnp.float32) * share_root[None, :]).astype(jnp.bfloat16)
    own_features = jnp.stack(from_all_reps(turned))
    other_features = across_cores(own_features)

    ring_row = chip // COLUMNS
    place = jnp.where(chip % COLUMNS == 0, ring_row, chips - 1 - ring_row)

    def pair_indices(distances):
        entries = []
        for distance in distances:
            at = (place + distance) % chips
            source = jnp.where(
                at < rows_of_chips, at * COLUMNS, (chips - 1 - at) * COLUMNS + 1
            )
            for target in range(2):
                offset = (source - chip - jnp.where(core == 0, target, 0)) % chips
                behind = (rep_index - offset // half_steps) % rep_size
                entries.append(behind * half_steps + offset % half_steps)
        return jnp.stack(entries).astype(jnp.int32)

    pair_cost = 2 * slot_total * 128 * 128 * share_width * 2
    sums_shape = jax.ShapeDtypeStruct((2, slab_rows, share_width), jnp.float32)

    def add_slabs(distances, slabs, sums):
        first = sums is None
        operands = [pair_indices(distances), fact_a, fact_b, words_a, words_b, *slabs]
        specs = [SMEM] * 3 + [VMEM] * (2 + len(slabs))
        aliases = {}
        if not first:
            aliases = {len(operands): 0}
            operands.append(sums)
            specs.append(VMEM)
        return pl.pallas_call(
            functools.partial(step_kernel, len(slabs), slot_total, first),
            out_shape=sums_shape,
            in_specs=specs,
            out_specs=VMEM,
            input_output_aliases=aliases,
            compiler_params=PARAMS,
            cost_estimate=pl.CostEstimate(
                flops=pair_cost * len(slabs), bytes_accessed=4 << 20, transcendentals=0
            ),
            name="add_slabs",
        )(*operands)

    sums = None
    distances, slabs = [0], [scaled]
    for step in range(1, chips // 2):
        distances += [-step, step]
        slabs += [forward, backward]
        if step + 1 < chips // 2:
            if len(slabs) > 4:
                sums = add_slabs(distances, slabs, sums)
                distances, slabs = [], []
            forward, backward = along_ring(forward, 1), along_ring(backward, -1)
        else:
            forward, sums = lax.optimization_barrier((forward, sums))
            forward = along_ring(forward, 1)
    sums = add_slabs(distances, slabs, sums)

    order = (rep_index - jnp.arange(rep_size, dtype=jnp.int32)) % rep_size
    order = jnp.concatenate([order, core[None]]).astype(jnp.int32)
    slab_shape = jax.ShapeDtypeStruct((slab_rows, share_width), jnp.float32)
    half_term = jax.ShapeDtypeStruct((width // 2, share_width), jnp.float32)
    own_sums, other_sums, keep, send = pl.pallas_call(
        functools.partial(last_kernel, slot_total, rep_size),
        out_shape=(slab_shape, slab_shape, half_term, half_term),
        in_specs=[SMEM] * 4 + [VMEM] * 6,
        out_specs=(VMEM,) * 4,
        scratch_shapes=[
            pltpu.VMEM(sums_shape.shape, jnp.float32),
            pltpu.VMEM((width, share_width), jnp.float32),
        ],
        compiler_params=PARAMS,
        name="last_step",
    )(
        pair_indices([chips // 2]), order, fact_a, fact_b, words_a, words_b, forward, sums,
        own_features, other_features,
    )

    def add_across_rows(total, distance):
        total = total.astype(jnp.bfloat16)
        return total.astype(jnp.float32) + across_rows(total, distance).astype(jnp.float32)

    total = keep + across_cores(send)
    own_sums = own_sums + across_cores(other_sums)
    aggregated = (own_sums * inverse_root[:, None]).astype(jnp.bfloat16)
    total = add_across_rows(total, 1)
    total, aggregated = lax.optimization_barrier((total, aggregated))
    parts = []
    for d in range(rep_size):
        rows_to = ((rep_index + d) % rep_size) * share_rows
        part = lax.dynamic_slice_in_dim(aggregated, rows_to, share_rows, 0)
        parts.append(along_rep(part, d) if d else part)
    distance = 2
    while distance < rows_of_chips:
        total = add_across_rows(total, distance)
        distance *= 2
    total = total.astype(jnp.bfloat16)
    total = total.astype(jnp.float32) + across_columns(total).astype(jnp.float32)
    total, parts = lax.optimization_barrier((total, parts))
    result = jnp.zeros((share_rows, width), jnp.float32)
    for d, part in enumerate(parts):
        columns_at = ((rep_index - d) % rep_size) * share_width
        side = lax.dynamic_slice_in_dim(weight, columns_at, share_width, 1)
        result = result + lax.dot_general(
            part, side, (((1,), (1,)), ((), ())), preferred_element_type=jnp.float32
        )
    input_grad = result.astype(jnp.bfloat16)
    weight_half = jnp.zeros((width // 2, width), jnp.float32)
    for d, columns in enumerate(from_all_reps(total)):
        at = ((rep_index - d) % rep_size) * share_width
        weight_half = lax.dynamic_update_slice_in_dim(weight_half, columns, at, 1)
    weight_half = weight_half * (1.0 / math.sqrt(slab_rows * blk_size))
    weight_half, input_grad = lax.optimization_barrier((weight_half, input_grad))
    other_half = across_cores(weight_half)
    weight_grad = jnp.concatenate(
        [jnp.where(core == 0, weight_half, other_half), jnp.where(core == 0, other_half, weight_half)]
    )
    return (input_grad, weight_grad)


def solution(mesh):
    return jax.shard_map(
        per_device,
        mesh=mesh,
        in_specs=(
            P(("blk", "rep"), None),
            P("blk", None),
            P(),
            P("blk", "rep", None, None, None),
            P("blk", "rep", None, None),
            P("blk", "rep"),
            P("blk"),
        ),
        out_specs=(P(("blk", "rep"), None), P()),
        check_vma=False,
    )
```

```python
import functools
import math

import jax
import jax.numpy as jnp
from jax import lax
from jax.experimental import pallas as pl
from jax.experimental.pallas import tpu as pltpu
from jax.sharding import PartitionSpec as P

CORES = 2
COLUMNS = 2


def device_of(row, column, core):
    return (row * COLUMNS + column) * CORES + core


def places(blk_size):
    rows = blk_size // (COLUMNS * CORES)
    return [(z, x, c) for z in range(rows) for x in range(COLUMNS) for c in range(CORES)]


def ring_order(rows):
    return [(z, 0) for z in range(rows)] + [(z, 1) for z in reversed(range(rows))]


def along_ring(block, distance):
    rows = lax.axis_size("blk") // (COLUMNS * CORES)
    order = ring_order(rows)
    route = []
    for place, (z, x) in enumerate(order):
        to_z, to_x = order[(place + distance) % len(order)]
        route += [(device_of(z, x, c), device_of(to_z, to_x, c)) for c in range(CORES)]
    return lax.ppermute(block, "blk", route)


def across_rows(block, distance):
    route = [
        (device_of(z, x, c), device_of(z ^ distance, x, c))
        for z, x, c in places(lax.axis_size("blk"))
    ]
    return lax.ppermute(block, "blk", route)


def across_columns(block):
    route = [
        (device_of(z, x, c), device_of(z, 1 - x, c)) for z, x, c in places(lax.axis_size("blk"))
    ]
    return lax.ppermute(block, "blk", route)


def across_cores(block):
    route = [
        (device_of(z, x, c), device_of(z, x, 1 - c)) for z, x, c in places(lax.axis_size("blk"))
    ]
    return lax.ppermute(block, "blk", route)


def along_rep(block, distance):
    size = lax.axis_size("rep")
    return lax.ppermute(block, "rep", [(i, (i + distance) % size) for i in range(size)])


def along_rep(block, distance):
    size = lax.axis_size("rep")
    return lax.ppermute(block, "rep", [(i, (i + distance) % size) for i in range(size)])


def across_columns_and_rep(block, distance):
    size = lax.axis_size("rep")
    route = [
        (device_of(z, x, c) * size + r, device_of(z, 1 - x, c) * size + (r + distance) % size)
        for z, x, c in places(lax.axis_size("blk"))
        for r in range(size)
    ]
    return lax.ppermute(block, ("blk", "rep"), route)


def from_all_reps(block):
    return [block] + [along_rep(block, d) for d in range(1, lax.axis_size("rep"))]


def add_pairs(plan, table_ref, first_slab, own_pieces, other_pieces, slabs, sums_ref):
    bit_ids = lax.broadcasted_iota(jnp.int32, (16, 8, 128), 1)
    for slab_id, slab_ref in enumerate(slabs):
        for target, pieces in enumerate((own_pieces, other_pieces)):
            at = plan.facts_size + 2 * (2 * (first_slab + slab_id) + target)
            piece, pair = table_ref[at], table_ref[at + 1]
            base = ((piece * 2 + target) * plan.pairs + pair) * plan.facts
            live_count = table_ref[base]
            for slot in range(plan.slots):
                row_block = table_ref[base + 1 + slot]
                column_block = table_ref[base + 1 + plan.slots + slot]
                word_rows = pl.ds(pl.multiple_of(pair * plan.pair_rows + slot * 16, 16), 16)
                slot_words = jnp.zeros((16, 128), jnp.float32)
                for piece_id, piece_ref in enumerate(pieces):
                    chosen = jnp.logical_and(piece == piece_id, slot < live_count)
                    scale = jnp.where(chosen, 1.0, 0.0)
                    slot_words += piece_ref[word_rows, :].astype(jnp.float32) * scale
                slot_words = slot_words.astype(jnp.int32)
                bits = jnp.bitwise_and(jnp.right_shift(slot_words[:, None, :], bit_ids), 1)
                transposed = bits.reshape(128, 128).astype(jnp.float32).astype(jnp.bfloat16)
                rows = pl.ds(pl.multiple_of(row_block * 128, 128), 128)
                columns = pl.ds(pl.multiple_of(column_block * 128, 128), 128)
                sums_ref[target, columns, :] += jnp.dot(
                    transposed, slab_ref[rows, :], preferred_element_type=jnp.float32
                )


def first_kernel(plan, slab_total, table_ref, *refs):
    pieces, slabs, sums_ref = refs[: 2 * plan.reps], refs[2 * plan.reps : -1], refs[-1]
    sums_ref[...] = jnp.zeros_like(sums_ref)
    add_pairs(plan, table_ref, 0, pieces[: plan.reps], pieces[plan.reps :], slabs, sums_ref)


def last_kernel(plan, last_slab, table_ref, *refs):
    own_pieces, other_pieces = refs[: plan.reps], refs[plan.reps : 2 * plan.reps]
    own_features, other_features = refs[2 * plan.reps : 3 * plan.reps], refs[3 * plan.reps : 4 * plan.reps]
    slab_ref, sums_in, own_ref, other_ref, keep_ref, send_ref, sums_ref, term_ref = refs[4 * plan.reps :]
    sums_ref[...] = sums_in[...]
    add_pairs(plan, table_ref, last_slab, own_pieces, other_pieces, [slab_ref], sums_ref)
    own_ref[...] = sums_ref[0]
    other_ref[...] = sums_ref[1]
    share = sums_ref.shape[1] // plan.reps
    width = term_ref.shape[0]
    order_at = plan.facts_size + 4 * (last_slab + 1)
    term = jnp.zeros(term_ref.shape, jnp.float32)
    for target, pieces in enumerate((own_features, other_features)):
        for piece_id, piece_ref in enumerate(pieces):
            start = pl.multiple_of(table_ref[order_at + piece_id] * share, share)
            for block in range(share // 128):
                rows = pl.ds(pl.multiple_of(start + block * 128, 128), 128)
                part = sums_ref[target, rows, :].astype(jnp.bfloat16)
                features = piece_ref[block * width : (block + 1) * width, :]
                term += jnp.dot(features, part, preferred_element_type=jnp.float32)
    term_ref[...] = term
    half = width // 2
    core = table_ref[order_at + plan.reps]
    keep_ref[...] = term_ref[pl.ds(pl.multiple_of(core * half, half), half), :]
    send_ref[...] = term_ref[pl.ds(pl.multiple_of((1 - core) * half, half), half), :]


class Plan:
    def __init__(self, reps, slots, pairs):
        self.reps, self.slots, self.pairs = reps, slots, pairs
        self.pair_rows = slots * 16 + 16
        self.facts = 1 + 2 * slots
        self.facts_size = reps * 2 * pairs * self.facts


def scale_kernel(share_width, degrees_hbm, gradient_hbm, scaled_ref, degrees_ref, rows_ref, semaphores):
    start = pl.multiple_of(lax.axis_index("rep") * share_width, share_width)
    chunks = semaphores.shape[0] - 1
    chunk_rows = rows_ref.shape[0] // chunks
    degrees_copy = pltpu.make_async_copy(degrees_hbm, degrees_ref, semaphores.at[chunks])
    degrees_copy.start()
    copies = []
    for chunk in range(chunks):
        rows = pl.ds(chunk * chunk_rows, chunk_rows)
        copies.append(
            pltpu.make_async_copy(gradient_hbm.at[rows], rows_ref.at[rows], semaphores.at[chunk])
        )
        copies[-1].start()
    degrees_copy.wait()
    roots = lax.rsqrt(degrees_ref[...].astype(jnp.float32))
    for chunk in range(chunks):
        copies[chunk].wait()
        for at in range(chunk * chunk_rows, (chunk + 1) * chunk_rows, 128):
            row = at // 128
            by_row = jnp.broadcast_to(roots[row : row + 1, :], (128, 128)).T
            for column in range(0, share_width, 128):
                own = pl.ds(pl.multiple_of(start + column, 128), 128)
                part = rows_ref[at : at + 128, own].astype(jnp.float32) * by_row
                scaled_ref[at : at + 128, column : column + 128] = part.astype(scaled_ref.dtype)


def payload_kernel(plan, facts_ref, words_ref, features_ref, roots_ref, pairs_ref, turned_ref):
    word_rows = plan.slots * 16
    for step in range(2 * plan.pairs):
        start = ((step % 2) * plan.pairs + step // 2) * plan.pair_rows
        words = words_ref[step].astype(jnp.float32).astype(pairs_ref.dtype)
        pairs_ref[start : start + word_rows, :] = words
        facts = jnp.broadcast_to(facts_ref[step : step + 1, :].astype(jnp.float32), (16, 128))
        pairs_ref[start + word_rows : start + plan.pair_rows, :] = facts.astype(pairs_ref.dtype)
    rows, width = features_ref.shape
    for block in range(rows // 128):
        part = features_ref[block * 128 : (block + 1) * 128, :].astype(jnp.float32).T
        part = part * roots_ref[:, block * 128 : (block + 1) * 128]
        turned_ref[block * width : (block + 1) * width, :] = part.astype(turned_ref.dtype)


SMEM = pl.BlockSpec(memory_space=pltpu.SMEM)
VMEM = pl.BlockSpec(memory_space=pltpu.VMEM)
PARAMS = pltpu.CompilerParams(vmem_limit_bytes=12 * 1024 * 1024)


def per_device(features, out_grad, weight, block_words, block_coords, block_counts, degrees):
    slab_rows, width = out_grad.shape
    rep_size = lax.axis_size("rep")
    blk_size = lax.axis_size("blk")
    chips = blk_size // CORES
    rows_of_chips = chips // COLUMNS
    rep_index = lax.axis_index("rep")
    blk_index = lax.axis_index("blk")
    core = blk_index % CORES
    chip = blk_index // CORES
    share_width = width // rep_size
    share_rows = slab_rows // rep_size
    slot_total = block_words.shape[2]
    half_steps = block_words.shape[1] // 2

    inverse_root = lax.rsqrt(degrees.astype(jnp.float32))
    if share_width % 128 == 0 and slab_rows % 1024 == 0:
        scaled = pl.pallas_call(
            functools.partial(scale_kernel, share_width),
            out_shape=jax.ShapeDtypeStruct((slab_rows, share_width), jnp.bfloat16),
            in_specs=[pl.BlockSpec(memory_space=pltpu.HBM)] * 2,
            out_specs=VMEM,
            scratch_shapes=[
                pltpu.VMEM((slab_rows // 128, 128), jnp.int32),
                pltpu.VMEM((slab_rows, width), jnp.bfloat16),
                pltpu.SemaphoreType.DMA((5,)),
            ],
            compiler_params=pltpu.CompilerParams(vmem_limit_bytes=60 * 1024 * 1024),
            name="scale",
        )(degrees.reshape(slab_rows // 128, 128), out_grad)
    else:
        own_columns = lax.dynamic_slice_in_dim(out_grad, rep_index * share_width, share_width, 1)
        scaled = (own_columns.astype(jnp.float32) * inverse_root[:, None]).astype(jnp.bfloat16)

    forward, backward = along_ring(scaled, 1), along_ring(scaled, -1)

    block_words, features, _ = lax.optimization_barrier((block_words, features, scaled))
    plan = Plan(rep_size, slot_total, half_steps)
    facts = jnp.concatenate(
        [block_counts[0][:, None], block_coords[0].reshape(2 * half_steps, 2 * slot_total)], axis=1
    )
    facts = jnp.pad(facts, ((0, 0), (0, 128 - plan.facts)))
    words_rows = half_steps * plan.pair_rows
    share_root = lax.dynamic_slice_in_dim(inverse_root, rep_index * share_rows, share_rows, 0)
    pairs, turned = pl.pallas_call(
        functools.partial(payload_kernel, plan),
        out_shape=(
            jax.ShapeDtypeStruct((2 * words_rows, 128), jnp.bfloat16),
            jax.ShapeDtypeStruct((share_rows // 128 * width, 128), jnp.bfloat16),
        ),
        in_specs=[VMEM] * 4,
        out_specs=(VMEM, VMEM),
        compiler_params=PARAMS,
        name="payload",
    )(facts, block_words[0].reshape(2 * half_steps, slot_total * 16, 128), features, share_root[None])
    own_pieces = from_all_reps(pairs)
    other_pieces = [across_cores(piece[words_rows:]) for piece in own_pieces]
    own_features = from_all_reps(turned)
    other_features = [across_cores(piece) for piece in own_features]

    def facts_of(piece):
        rows = piece[:words_rows].reshape(half_steps, plan.pair_rows, 128)[:, slot_total * 16]
        return rows[:, : plan.facts].astype(jnp.int32).reshape(-1)

    ring_row = chip // COLUMNS
    place = jnp.where(chip % COLUMNS == 0, ring_row, chips - 1 - ring_row)
    distances = [0]
    for step in range(1, chips // 2):
        distances += [-step, step]
    distances.append(chips // 2)
    entries = []
    for distance in distances:
        at = (place + distance) % chips
        source = jnp.where(at < rows_of_chips, at * COLUMNS, (chips - 1 - at) * COLUMNS + 1)
        for target in range(2):
            offset = (source - chip - jnp.where(core == 0, target, 0)) % chips
            entries += [(rep_index - offset // half_steps) % rep_size, offset % half_steps]
    entries += [(rep_index - d) % rep_size for d in range(rep_size)] + [core]
    table = [facts_of(piece) for pair in zip(own_pieces, other_pieces) for piece in pair]
    table = jnp.concatenate(table + [jnp.stack(entries).astype(jnp.int32)])

    slabs = [scaled]
    for step in range(1, chips // 2):
        slabs += [forward, backward]
        forward, backward = along_ring(forward, 1), along_ring(backward, -1)
    del backward

    slab_shape = jax.ShapeDtypeStruct((slab_rows, share_width), jnp.float32)
    half_term = jax.ShapeDtypeStruct((width // 2, share_width), jnp.float32)
    sums_shape = jax.ShapeDtypeStruct((2, slab_rows, share_width), jnp.float32)
    pair_flops = 2 * slot_total * 128 * 128 * share_width * 2
    sums = pl.pallas_call(
        functools.partial(first_kernel, plan, len(slabs)),
        out_shape=sums_shape,
        in_specs=[SMEM] + [VMEM] * (2 * rep_size + len(slabs)),
        out_specs=VMEM,
        compiler_params=PARAMS,
        cost_estimate=pl.CostEstimate(flops=1, bytes_accessed=1, transcendentals=0),
        name="first_slabs",
    )(table, *own_pieces, *other_pieces, *slabs)
    own_sums, other_sums, keep, send = pl.pallas_call(
        functools.partial(last_kernel, plan, len(slabs)),
        out_shape=(slab_shape, slab_shape, half_term, half_term),
        in_specs=[SMEM] + [VMEM] * (4 * rep_size + 2),
        out_specs=(VMEM,) * 4,
        scratch_shapes=[
            pltpu.VMEM(sums_shape.shape, jnp.float32),
            pltpu.VMEM((width, share_width), jnp.float32),
        ],
        compiler_params=PARAMS,
        name="last_slab",
    )(table, *own_pieces, *other_pieces, *own_features, *other_features, forward, sums)

    def add_across_rows(total, distance):
        total = total.astype(jnp.bfloat16)
        return total.astype(jnp.float32) + across_rows(total, distance).astype(jnp.float32)

    total = keep + across_cores(send)
    own_sums = own_sums + across_cores(other_sums)
    aggregated = (own_sums * inverse_root[:, None]).astype(jnp.bfloat16)
    distance = 1
    while distance < rows_of_chips:
        total = add_across_rows(total, distance)
        distance *= 2
    total, aggregated = lax.optimization_barrier((total, aggregated))
    total = total.astype(jnp.bfloat16)
    total = total.astype(jnp.float32) + across_columns(total).astype(jnp.float32)

    total = total.astype(jnp.bfloat16)
    result = jnp.zeros((share_rows, width), jnp.float32)
    weight_half = jnp.zeros((width // 2, width), jnp.float32)
    for d in range(rep_size):
        rows_to = ((rep_index + d) % rep_size) * share_rows
        part = lax.dynamic_slice_in_dim(aggregated, rows_to, share_rows, 0)
        columns = total
        if d:
            both = along_rep(jnp.concatenate([part, total]), d)
            part, columns = both[:share_rows], both[share_rows:]
        columns_at = ((rep_index - d) % rep_size) * share_width
        side = lax.dynamic_slice_in_dim(weight, columns_at, share_width, 1)
        result = result + lax.dot_general(
            part, side, (((1,), (1,)), ((), ())), preferred_element_type=jnp.float32
        )
        weight_half = lax.dynamic_update_slice_in_dim(
            weight_half, columns.astype(jnp.float32), columns_at, 1
        )
    input_grad = result.astype(jnp.bfloat16)
    weight_half = weight_half * (1.0 / math.sqrt(slab_rows * blk_size))
    other_half = across_cores(weight_half)
    weight_grad = jnp.concatenate(
        [jnp.where(core == 0, weight_half, other_half), jnp.where(core == 0, other_half, weight_half)]
    )
    return (input_grad, weight_grad)


def solution(mesh):
    return jax.shard_map(
        per_device,
        mesh=mesh,
        in_specs=(
            P(("blk", "rep"), None),
            P("blk", None),
            P(),
            P("blk", "rep", None, None, None),
            P("blk", "rep", None, None),
            P("blk", "rep"),
            P("blk"),
        ),
        out_specs=(P(("blk", "rep"), None), P()),
        check_vma=False,
    )
```

```python
import functools
import math

import jax
import jax.numpy as jnp
from jax import lax
from jax.experimental import pallas as pl
from jax.experimental.pallas import tpu as pltpu
from jax.sharding import PartitionSpec as P

CORES = 2
COLUMNS = 2


def device_of(row, column, core):
    return (row * COLUMNS + column) * CORES + core


def places(blk_size):
    rows = blk_size // (COLUMNS * CORES)
    return [(z, x, c) for z in range(rows) for x in range(COLUMNS) for c in range(CORES)]


def ring_order(rows):
    return [(z, 0) for z in range(rows)] + [(z, 1) for z in reversed(range(rows))]


def along_ring(block, distance):
    rows = lax.axis_size("blk") // (COLUMNS * CORES)
    order = ring_order(rows)
    route = []
    for place, (z, x) in enumerate(order):
        to_z, to_x = order[(place + distance) % len(order)]
        route += [(device_of(z, x, c), device_of(to_z, to_x, c)) for c in range(CORES)]
    return lax.ppermute(block, "blk", route)


def across(block, rows=0, columns=0, reps=0):
    size = lax.axis_size("rep")
    route = [
        (device_of(z, x, c), device_of(z ^ rows, x ^ columns, c))
        for z, x, c in places(lax.axis_size("blk"))
    ]
    if not reps:
        return lax.ppermute(block, "blk", route)
    route = [(a * size + r, b * size + (r + reps) % size) for a, b in route for r in range(size)]
    return lax.ppermute(block, ("blk", "rep"), route)


def across_cores(block):
    route = [
        (device_of(z, x, c), device_of(z, x, 1 - c)) for z, x, c in places(lax.axis_size("blk"))
    ]
    return lax.ppermute(block, "blk", route)


def along_rep(block, distance):
    size = lax.axis_size("rep")
    return lax.ppermute(block, "rep", [(i, (i + distance) % size) for i in range(size)])


def along_rep(block, distance):
    size = lax.axis_size("rep")
    return lax.ppermute(block, "rep", [(i, (i + distance) % size) for i in range(size)])


def across_columns_and_rep(block, distance):
    size = lax.axis_size("rep")
    route = [
        (device_of(z, x, c) * size + r, device_of(z, 1 - x, c) * size + (r + distance) % size)
        for z, x, c in places(lax.axis_size("blk"))
        for r in range(size)
    ]
    return lax.ppermute(block, ("blk", "rep"), route)


def from_all_reps(block):
    return [block] + [along_rep(block, d) for d in range(1, lax.axis_size("rep"))]


def add_pairs(plan, table_ref, first_slab, own_pieces, other_pieces, slabs, sums_ref):
    bit_ids = lax.broadcasted_iota(jnp.int32, (16, 8, 128), 1)
    for slab_id, slab_ref in enumerate(slabs):
        for target, pieces in enumerate((own_pieces, other_pieces)):
            at = plan.facts_size + 2 * (2 * (first_slab + slab_id) + target)
            piece, pair = table_ref[at], table_ref[at + 1]
            base = ((piece * 2 + target) * plan.pairs + pair) * plan.facts
            live_count = table_ref[base]
            for slot in range(plan.slots):
                row_block = table_ref[base + 1 + slot]
                column_block = table_ref[base + 1 + plan.slots + slot]
                word_rows = pl.ds(pl.multiple_of(pair * plan.pair_rows + slot * 16, 16), 16)
                slot_words = jnp.zeros((16, 128), jnp.float32)
                for piece_id, piece_ref in enumerate(pieces):
                    chosen = jnp.logical_and(piece == piece_id, slot < live_count)
                    scale = jnp.where(chosen, 1.0, 0.0)
                    slot_words += piece_ref[word_rows, :].astype(jnp.float32) * scale
                slot_words = slot_words.astype(jnp.int32)
                bits = jnp.bitwise_and(jnp.right_shift(slot_words[:, None, :], bit_ids), 1)
                transposed = bits.reshape(128, 128).astype(jnp.float32).astype(jnp.bfloat16)
                rows = pl.ds(pl.multiple_of(row_block * 128, 128), 128)
                columns = pl.ds(pl.multiple_of(column_block * 128, 128), 128)
                sums_ref[target, columns, :] += jnp.dot(
                    transposed, slab_ref[rows, :], preferred_element_type=jnp.float32
                )


def first_kernel(plan, slab_total, table_ref, *refs):
    pieces, slabs, sums_ref = refs[: 2 * plan.reps], refs[2 * plan.reps : -1], refs[-1]
    sums_ref[...] = jnp.zeros_like(sums_ref)
    add_pairs(plan, table_ref, 0, pieces[: plan.reps], pieces[plan.reps :], slabs, sums_ref)


def last_kernel(plan, last_slab, table_ref, *refs):
    own_pieces, other_pieces = refs[: plan.reps], refs[plan.reps : 2 * plan.reps]
    own_features, other_features = refs[2 * plan.reps : 3 * plan.reps], refs[3 * plan.reps : 4 * plan.reps]
    slab_ref, sums_in, own_ref, other_ref, keep_ref, send_ref, sums_ref, term_ref = refs[4 * plan.reps :]
    sums_ref[...] = sums_in[...]
    add_pairs(plan, table_ref, last_slab, own_pieces, other_pieces, [slab_ref], sums_ref)
    own_ref[...] = sums_ref[0]
    other_ref[...] = sums_ref[1]
    share = sums_ref.shape[1] // plan.reps
    width = term_ref.shape[0]
    order_at = plan.facts_size + 4 * (last_slab + 1)
    term = jnp.zeros(term_ref.shape, jnp.float32)
    for target, pieces in enumerate((own_features, other_features)):
        for piece_id, piece_ref in enumerate(pieces):
            start = pl.multiple_of(table_ref[order_at + piece_id] * share, share)
            for block in range(share // 128):
                rows = pl.ds(pl.multiple_of(start + block * 128, 128), 128)
                part = sums_ref[target, rows, :].astype(jnp.bfloat16)
                features = piece_ref[block * width : (block + 1) * width, :]
                term += jnp.dot(features, part, preferred_element_type=jnp.float32)
    term_ref[...] = term
    half = width // 2
    core = table_ref[order_at + plan.reps]
    keep_ref[...] = term_ref[pl.ds(pl.multiple_of(core * half, half), half), :]
    send_ref[...] = term_ref[pl.ds(pl.multiple_of((1 - core) * half, half), half), :]


class Plan:
    def __init__(self, reps, slots, pairs):
        self.reps, self.slots, self.pairs = reps, slots, pairs
        self.pair_rows = slots * 16 + 16
        self.facts = 1 + 2 * slots
        self.facts_size = reps * 2 * pairs * self.facts


def scale_kernel(share_width, degrees_hbm, gradient_hbm, scaled_ref, degrees_ref, rows_ref, semaphores):
    start = pl.multiple_of(lax.axis_index("rep") * share_width, share_width)
    chunks = semaphores.shape[0] - 1
    chunk_rows = rows_ref.shape[0] // chunks
    degrees_copy = pltpu.make_async_copy(degrees_hbm, degrees_ref, semaphores.at[chunks])
    degrees_copy.start()
    copies = []
    for chunk in range(chunks):
        rows = pl.ds(chunk * chunk_rows, chunk_rows)
        copies.append(
            pltpu.make_async_copy(gradient_hbm.at[rows], rows_ref.at[rows], semaphores.at[chunk])
        )
        copies[-1].start()
    degrees_copy.wait()
    roots = lax.rsqrt(degrees_ref[...].astype(jnp.float32))
    for chunk in range(chunks):
        copies[chunk].wait()
        for at in range(chunk * chunk_rows, (chunk + 1) * chunk_rows, 128):
            row = at // 128
            by_row = jnp.broadcast_to(roots[row : row + 1, :], (128, 128)).T
            for column in range(0, share_width, 128):
                own = pl.ds(pl.multiple_of(start + column, 128), 128)
                part = rows_ref[at : at + 128, own].astype(jnp.float32) * by_row
                scaled_ref[at : at + 128, column : column + 128] = part.astype(scaled_ref.dtype)


def payload_kernel(plan, facts_ref, words_ref, features_ref, roots_ref, pairs_ref, turned_ref):
    word_rows = plan.slots * 16
    for step in range(2 * plan.pairs):
        start = ((step % 2) * plan.pairs + step // 2) * plan.pair_rows
        words = words_ref[step].astype(jnp.float32).astype(pairs_ref.dtype)
        pairs_ref[start : start + word_rows, :] = words
        facts = jnp.broadcast_to(facts_ref[step : step + 1, :].astype(jnp.float32), (16, 128))
        pairs_ref[start + word_rows : start + plan.pair_rows, :] = facts.astype(pairs_ref.dtype)
    rows, width = features_ref.shape
    for block in range(rows // 128):
        part = features_ref[block * 128 : (block + 1) * 128, :].astype(jnp.float32).T
        part = part * roots_ref[:, block * 128 : (block + 1) * 128]
        turned_ref[block * width : (block + 1) * width, :] = part.astype(turned_ref.dtype)


SMEM = pl.BlockSpec(memory_space=pltpu.SMEM)
VMEM = pl.BlockSpec(memory_space=pltpu.VMEM)
PARAMS = pltpu.CompilerParams(vmem_limit_bytes=12 * 1024 * 1024)


def per_device(features, out_grad, weight, block_words, block_coords, block_counts, degrees):
    slab_rows, width = out_grad.shape
    rep_size = lax.axis_size("rep")
    blk_size = lax.axis_size("blk")
    chips = blk_size // CORES
    rows_of_chips = chips // COLUMNS
    rep_index = lax.axis_index("rep")
    blk_index = lax.axis_index("blk")
    core = blk_index % CORES
    chip = blk_index // CORES
    share_width = width // rep_size
    share_rows = slab_rows // rep_size
    slot_total = block_words.shape[2]
    half_steps = block_words.shape[1] // 2

    inverse_root = lax.rsqrt(degrees.astype(jnp.float32))
    if share_width % 128 == 0 and slab_rows % 1024 == 0:
        scaled = pl.pallas_call(
            functools.partial(scale_kernel, share_width),
            out_shape=jax.ShapeDtypeStruct((slab_rows, share_width), jnp.bfloat16),
            in_specs=[pl.BlockSpec(memory_space=pltpu.HBM)] * 2,
            out_specs=VMEM,
            scratch_shapes=[
                pltpu.VMEM((slab_rows // 128, 128), jnp.int32),
                pltpu.VMEM((slab_rows, width), jnp.bfloat16),
                pltpu.SemaphoreType.DMA((5,)),
            ],
            compiler_params=pltpu.CompilerParams(vmem_limit_bytes=60 * 1024 * 1024),
            name="scale",
        )(degrees.reshape(slab_rows // 128, 128), out_grad)
    else:
        own_columns = lax.dynamic_slice_in_dim(out_grad, rep_index * share_width, share_width, 1)
        scaled = (own_columns.astype(jnp.float32) * inverse_root[:, None]).astype(jnp.bfloat16)

    forward, backward = along_ring(scaled, 1), along_ring(scaled, -1)

    block_words, features, _ = lax.optimization_barrier((block_words, features, scaled))
    plan = Plan(rep_size, slot_total, half_steps)
    facts = jnp.concatenate(
        [block_counts[0][:, None], block_coords[0].reshape(2 * half_steps, 2 * slot_total)], axis=1
    )
    facts = jnp.pad(facts, ((0, 0), (0, 128 - plan.facts)))
    words_rows = half_steps * plan.pair_rows
    share_root = lax.dynamic_slice_in_dim(inverse_root, rep_index * share_rows, share_rows, 0)
    pairs, turned = pl.pallas_call(
        functools.partial(payload_kernel, plan),
        out_shape=(
            jax.ShapeDtypeStruct((2 * words_rows, 128), jnp.bfloat16),
            jax.ShapeDtypeStruct((share_rows // 128 * width, 128), jnp.bfloat16),
        ),
        in_specs=[VMEM] * 4,
        out_specs=(VMEM, VMEM),
        compiler_params=PARAMS,
        name="payload",
    )(facts, block_words[0].reshape(2 * half_steps, slot_total * 16, 128), features, share_root[None])
    own_pieces = from_all_reps(pairs)
    other_pieces = [across_cores(piece[words_rows:]) for piece in own_pieces]
    own_features = from_all_reps(turned)
    other_features = [across_cores(piece) for piece in own_features]

    def facts_of(piece):
        rows = piece[:words_rows].reshape(half_steps, plan.pair_rows, 128)[:, slot_total * 16]
        return rows[:, : plan.facts].astype(jnp.int32).reshape(-1)

    ring_row = chip // COLUMNS
    place = jnp.where(chip % COLUMNS == 0, ring_row, chips - 1 - ring_row)
    distances = [0]
    for step in range(1, chips // 2):
        distances += [-step, step]
    distances.append(chips // 2)
    entries = []
    for distance in distances:
        at = (place + distance) % chips
        source = jnp.where(at < rows_of_chips, at * COLUMNS, (chips - 1 - at) * COLUMNS + 1)
        for target in range(2):
            offset = (source - chip - jnp.where(core == 0, target, 0)) % chips
            entries += [(rep_index - offset // half_steps) % rep_size, offset % half_steps]
    entries += [(rep_index - d) % rep_size for d in range(rep_size)] + [core]
    table = [facts_of(piece) for pair in zip(own_pieces, other_pieces) for piece in pair]
    table = jnp.concatenate(table + [jnp.stack(entries).astype(jnp.int32)])

    slabs = [scaled]
    for step in range(1, chips // 2):
        slabs += [forward, backward]
        forward, backward = along_ring(forward, 1), along_ring(backward, -1)
    del backward

    slab_shape = jax.ShapeDtypeStruct((slab_rows, share_width), jnp.float32)
    half_term = jax.ShapeDtypeStruct((width // 2, share_width), jnp.float32)
    sums_shape = jax.ShapeDtypeStruct((2, slab_rows, share_width), jnp.float32)
    pair_flops = 2 * slot_total * 128 * 128 * share_width * 2
    sums = pl.pallas_call(
        functools.partial(first_kernel, plan, len(slabs)),
        out_shape=sums_shape,
        in_specs=[SMEM] + [VMEM] * (2 * rep_size + len(slabs)),
        out_specs=VMEM,
        compiler_params=PARAMS,
        cost_estimate=pl.CostEstimate(flops=1, bytes_accessed=1, transcendentals=0),
        name="first_slabs",
    )(table, *own_pieces, *other_pieces, *slabs)
    own_sums, other_sums, keep, send = pl.pallas_call(
        functools.partial(last_kernel, plan, len(slabs)),
        out_shape=(slab_shape, slab_shape, half_term, half_term),
        in_specs=[SMEM] + [VMEM] * (4 * rep_size + 2),
        out_specs=(VMEM,) * 4,
        scratch_shapes=[
            pltpu.VMEM(sums_shape.shape, jnp.float32),
            pltpu.VMEM((width, share_width), jnp.float32),
        ],
        compiler_params=PARAMS,
        name="last_slab",
    )(table, *own_pieces, *other_pieces, *own_features, *other_features, forward, sums)

    def wide(values):
        return values.astype(jnp.float32)

    total = (keep + across_cores(send)).astype(jnp.bfloat16)
    own_sums = own_sums + across_cores(other_sums)
    aggregated = (own_sums * inverse_root[:, None]).astype(jnp.bfloat16)
    row_bits = [1 << bit for bit in range(rows_of_chips.bit_length() - 1)]
    total = (wide(total) + wide(across(total, rows=row_bits[0]))) + (
        wide(across(total, columns=1)) + wide(across(total, rows=row_bits[0], columns=1))
    )
    total = total.astype(jnp.bfloat16)
    for bit in row_bits[1:-1]:
        total = (wide(total) + wide(across(total, rows=bit))).astype(jnp.bfloat16)
    total, aggregated = lax.optimization_barrier((total, aggregated))
    result = jnp.zeros((share_rows, width), jnp.float32)
    weight_half = jnp.zeros((width // 2, width), jnp.float32)
    for d in range(rep_size):
        rows_to = ((rep_index + d) % rep_size) * share_rows
        part = lax.dynamic_slice_in_dim(aggregated, rows_to, share_rows, 0)
        columns = total
        far = across(total, rows=row_bits[-1], reps=d)
        if d:
            both = along_rep(jnp.concatenate([part, total]), d)
            part, columns = both[:share_rows], both[share_rows:]
        columns_at = ((rep_index - d) % rep_size) * share_width
        side = lax.dynamic_slice_in_dim(weight, columns_at, share_width, 1)
        result = result + lax.dot_general(
            part, side, (((1,), (1,)), ((), ())), preferred_element_type=jnp.float32
        )
        weight_half = lax.dynamic_update_slice_in_dim(
            weight_half, wide(columns) + wide(far), columns_at, 1
        )
    input_grad = result.astype(jnp.bfloat16)
    weight_half = weight_half * (1.0 / math.sqrt(slab_rows * blk_size))
    other_half = across_cores(weight_half)
    weight_grad = jnp.concatenate(
        [jnp.where(core == 0, weight_half, other_half), jnp.where(core == 0, other_half, weight_half)]
    )
    return (input_grad, weight_grad)


def solution(mesh):
    return jax.shard_map(
        per_device,
        mesh=mesh,
        in_specs=(
            P(("blk", "rep"), None),
            P("blk", None),
            P(),
            P("blk", "rep", None, None, None),
            P("blk", "rep", None, None),
            P("blk", "rep"),
            P("blk"),
        ),
        out_specs=(P(("blk", "rep"), None), P()),
        check_vma=False,
    )
```

```python
import functools
import math

import jax
import jax.numpy as jnp
from jax import lax
from jax.experimental import pallas as pl
from jax.experimental.pallas import tpu as pltpu
from jax.sharding import PartitionSpec as P

CORES = 2
COLUMNS = 2


def device_of(row, column, core):
    return (row * COLUMNS + column) * CORES + core


def places(blk_size):
    rows = blk_size // (COLUMNS * CORES)
    return [(z, x, c) for z in range(rows) for x in range(COLUMNS) for c in range(CORES)]


def ring_order(rows):
    return [(z, 0) for z in range(rows)] + [(z, 1) for z in reversed(range(rows))]


def along_ring(block, distance):
    rows = lax.axis_size("blk") // (COLUMNS * CORES)
    order = ring_order(rows)
    route = []
    for place, (z, x) in enumerate(order):
        to_z, to_x = order[(place + distance) % len(order)]
        route += [(device_of(z, x, c), device_of(to_z, to_x, c)) for c in range(CORES)]
    return lax.ppermute(block, "blk", route)


def across(block, *moves):
    size = lax.axis_size("rep")
    route = []
    for z, x, c in places(lax.axis_size("blk")):
        if moves[c] is not None:
            rows, columns, reps = moves[c]
            start, end = device_of(z, x, c), device_of(z ^ rows, x ^ columns, c)
            route += [(start * size + r, end * size + (r + reps) % size) for r in range(size)]
    return lax.ppermute(block, ("blk", "rep"), route)


def across_cores(block):
    route = [
        (device_of(z, x, c), device_of(z, x, 1 - c)) for z, x, c in places(lax.axis_size("blk"))
    ]
    return lax.ppermute(block, "blk", route)


def along_rep(block, distance):
    size = lax.axis_size("rep")
    return lax.ppermute(block, "rep", [(i, (i + distance) % size) for i in range(size)])


def along_rep(block, distance):
    size = lax.axis_size("rep")
    return lax.ppermute(block, "rep", [(i, (i + distance) % size) for i in range(size)])


def across_columns_and_rep(block, distance):
    size = lax.axis_size("rep")
    route = [
        (device_of(z, x, c) * size + r, device_of(z, 1 - x, c) * size + (r + distance) % size)
        for z, x, c in places(lax.axis_size("blk"))
        for r in range(size)
    ]
    return lax.ppermute(block, ("blk", "rep"), route)


def from_all_reps(block):
    return [block] + [along_rep(block, d) for d in range(1, lax.axis_size("rep"))]


def add_pairs(plan, table_ref, first_slab, own_pieces, other_pieces, slabs, sums):
    bit_ids = lax.broadcasted_iota(jnp.int32, (16, 8, 128), 1)
    for slab_id, slab_ref in enumerate(slabs):
        for target, pieces in enumerate((own_pieces, other_pieces)):
            at = plan.facts_size + 2 * (2 * (first_slab + slab_id) + target)
            piece, pair = table_ref[at], table_ref[at + 1]
            base = ((piece * 2 + target) * plan.pairs + pair) * plan.facts
            live_count = table_ref[base]
            for slot in range(plan.slots):
                row_block = table_ref[base + 1 + slot]
                column_block = table_ref[base + 1 + plan.slots + slot]
                word_rows = pl.ds(pl.multiple_of(pair * plan.pair_rows + slot * 16, 16), 16)
                slot_words = jnp.zeros((16, 128), jnp.float32)
                for piece_id, piece_ref in enumerate(pieces):
                    chosen = jnp.logical_and(piece == piece_id, slot < live_count)
                    scale = jnp.where(chosen, 1.0, 0.0)
                    slot_words += piece_ref[word_rows, :].astype(jnp.float32) * scale
                slot_words = slot_words.astype(jnp.int32)
                bits = jnp.bitwise_and(jnp.right_shift(slot_words[:, None, :], bit_ids), 1)
                transposed = bits.reshape(128, 128).astype(jnp.float32).astype(jnp.bfloat16)
                rows = pl.ds(pl.multiple_of(row_block * 128, 128), 128)
                columns = pl.ds(pl.multiple_of(column_block * 128, 128), 128)
                sums[target][columns, :] += jnp.dot(
                    transposed, slab_ref[rows, :], preferred_element_type=jnp.float32
                )


def adding_kernel(plan, first_slab, slab_total, table_ref, *refs):
    own_pieces, other_pieces = refs[: plan.reps], refs[plan.reps : 2 * plan.reps]
    slabs, sums_in, sums = refs[2 * plan.reps :][:slab_total], refs[2 * plan.reps + slab_total : -2], refs[-2:]
    for target, sums_ref in enumerate(sums):
        sums_ref[...] = sums_in[target][...] if sums_in else jnp.zeros_like(sums_ref)
    add_pairs(plan, table_ref, first_slab, own_pieces, other_pieces, slabs, sums)


def last_kernel(plan, last_slab, table_ref, *refs):
    own_pieces, other_pieces = refs[: plan.reps], refs[plan.reps : 2 * plan.reps]
    own_features, other_features = refs[2 * plan.reps : 3 * plan.reps], refs[3 * plan.reps : 4 * plan.reps]
    slab_ref, own_in, other_in, own_ref, other_ref, term_ref = refs[4 * plan.reps :]
    own_ref[...] = own_in[...]
    other_ref[...] = other_in[...]
    sums = (own_ref, other_ref)
    add_pairs(plan, table_ref, last_slab, own_pieces, other_pieces, [slab_ref], sums)
    share = own_ref.shape[0] // plan.reps
    order_at = plan.facts_size + 4 * (last_slab + 1)
    term = jnp.zeros(term_ref.shape, jnp.float32)
    for sums_ref, pieces in zip(sums, (own_features, other_features)):
        for piece_id, piece_ref in enumerate(pieces):
            rows = pl.ds(pl.multiple_of(table_ref[order_at + piece_id] * share, share), share)
            part = sums_ref[rows, :].astype(jnp.bfloat16)
            term += jnp.dot(piece_ref[...], part, preferred_element_type=jnp.float32)
    term_ref[...] = term.astype(term_ref.dtype)


class Plan:
    def __init__(self, reps, slots, pairs):
        self.reps, self.slots, self.pairs = reps, slots, pairs
        self.pair_rows = slots * 16 + 16
        self.facts = 1 + 2 * slots
        self.facts_size = reps * 2 * pairs * self.facts


def scale_kernel(share_width, degrees_hbm, gradient_hbm, scaled_ref, degrees_ref, rows_ref, semaphores):
    start = pl.multiple_of(lax.axis_index("rep") * share_width, share_width)
    chunks = semaphores.shape[0] - 1
    chunk_rows = rows_ref.shape[0] // chunks
    degrees_copy = pltpu.make_async_copy(degrees_hbm, degrees_ref, semaphores.at[chunks])
    degrees_copy.start()
    copies = []
    for chunk in range(chunks):
        rows = pl.ds(chunk * chunk_rows, chunk_rows)
        copies.append(
            pltpu.make_async_copy(gradient_hbm.at[rows], rows_ref.at[rows], semaphores.at[chunk])
        )
        copies[-1].start()
    degrees_copy.wait()
    roots = lax.rsqrt(degrees_ref[...].astype(jnp.float32))
    for chunk in range(chunks):
        copies[chunk].wait()
        for at in range(chunk * chunk_rows, (chunk + 1) * chunk_rows, 128):
            row = at // 128
            by_row = jnp.broadcast_to(roots[row : row + 1, :], (128, 128)).T
            for column in range(0, share_width, 128):
                own = pl.ds(pl.multiple_of(start + column, 128), 128)
                part = rows_ref[at : at + 128, own].astype(jnp.float32) * by_row
                scaled_ref[at : at + 128, column : column + 128] = part.astype(scaled_ref.dtype)


def payload_kernel(plan, facts_ref, words_ref, features_ref, roots_ref, pairs_ref, turned_ref):
    word_rows = plan.slots * 16
    for step in range(2 * plan.pairs):
        start = ((step % 2) * plan.pairs + step // 2) * plan.pair_rows
        words = words_ref[step].astype(jnp.float32).astype(pairs_ref.dtype)
        pairs_ref[start : start + word_rows, :] = words
        facts = jnp.broadcast_to(facts_ref[step : step + 1, :].astype(jnp.float32), (16, 128))
        pairs_ref[start + word_rows : start + plan.pair_rows, :] = facts.astype(pairs_ref.dtype)
    for at in range(0, features_ref.shape[0], 128):
        part = features_ref[at : at + 128, :].astype(jnp.float32).T * roots_ref[:, at : at + 128]
        turned_ref[:, at : at + 128] = part.astype(turned_ref.dtype)


SMEM = pl.BlockSpec(memory_space=pltpu.SMEM)
VMEM = pl.BlockSpec(memory_space=pltpu.VMEM)
COST = pl.CostEstimate(flops=1, bytes_accessed=1, transcendentals=0)
PARAMS = pltpu.CompilerParams(vmem_limit_bytes=12 * 1024 * 1024)


def in_hbm(block):
    return pltpu.with_memory_space_constraint(block, pltpu.HBM)


def per_device(features, out_grad, weight, block_words, block_coords, block_counts, degrees):
    slab_rows, width = out_grad.shape
    rep_size = lax.axis_size("rep")
    blk_size = lax.axis_size("blk")
    chips = blk_size // CORES
    rows_of_chips = chips // COLUMNS
    rep_index = lax.axis_index("rep")
    blk_index = lax.axis_index("blk")
    core = blk_index % CORES
    chip = blk_index // CORES
    share_width = width // rep_size
    share_rows = slab_rows // rep_size
    slot_total = block_words.shape[2]
    half_steps = block_words.shape[1] // 2

    inverse_root = lax.rsqrt(degrees.astype(jnp.float32))
    if share_width % 128 == 0 and slab_rows % 1024 == 0:
        scaled = pl.pallas_call(
            functools.partial(scale_kernel, share_width),
            out_shape=pltpu.VMEM((slab_rows, share_width), jnp.bfloat16),
            in_specs=[pl.BlockSpec(memory_space=pltpu.HBM)] * 2,
            out_specs=VMEM,
            scratch_shapes=[
                pltpu.VMEM((slab_rows // 128, 128), jnp.int32),
                pltpu.VMEM((slab_rows, width), jnp.bfloat16),
                pltpu.SemaphoreType.DMA((5,)),
            ],
            compiler_params=PARAMS,
            name="scale",
        )(in_hbm(degrees.reshape(slab_rows // 128, 128)), in_hbm(out_grad))
    else:
        own_columns = lax.dynamic_slice_in_dim(out_grad, rep_index * share_width, share_width, 1)
        scaled = (own_columns.astype(jnp.float32) * inverse_root[:, None]).astype(jnp.bfloat16)

    forward, backward = along_ring(scaled, 1), along_ring(scaled, -1)

    block_words, features, _ = lax.optimization_barrier((block_words, features, scaled))
    plan = Plan(rep_size, slot_total, half_steps)
    facts = jnp.concatenate(
        [block_counts[0][:, None], block_coords[0].reshape(2 * half_steps, 2 * slot_total)], axis=1
    )
    facts = jnp.pad(facts, ((0, 0), (0, 128 - plan.facts)))
    words_rows = half_steps * plan.pair_rows
    share_root = lax.dynamic_slice_in_dim(inverse_root, rep_index * share_rows, share_rows, 0)
    pairs, turned = pl.pallas_call(
        functools.partial(payload_kernel, plan),
        out_shape=(
            jax.ShapeDtypeStruct((2 * words_rows, 128), jnp.bfloat16),
            jax.ShapeDtypeStruct((width, share_rows), jnp.bfloat16),
        ),
        in_specs=[VMEM] * 4,
        out_specs=(VMEM, VMEM),
        compiler_params=PARAMS,
        cost_estimate=COST,
        name="payload",
    )(facts, block_words[0].reshape(2 * half_steps, slot_total * 16, 128), features, share_root[None])
    own_pieces = from_all_reps(pairs)
    other_pieces = [across_cores(piece[words_rows:]) for piece in own_pieces]
    own_features = from_all_reps(turned)
    other_features = [across_cores(piece) for piece in own_features]

    def facts_of(piece):
        rows = piece[:words_rows].reshape(half_steps, plan.pair_rows, 128)[:, slot_total * 16]
        return rows[:, : plan.facts].astype(jnp.int32).reshape(-1)

    ring_row = chip // COLUMNS
    place = jnp.where(chip % COLUMNS == 0, ring_row, chips - 1 - ring_row)
    distances = [0]
    for step in range(1, chips // 2):
        distances += [-step, step]
    distances.append(chips // 2)
    entries = []
    for distance in distances:
        at = (place + distance) % chips
        source = jnp.where(at < rows_of_chips, at * COLUMNS, (chips - 1 - at) * COLUMNS + 1)
        for target in range(2):
            offset = (source - chip - jnp.where(core == 0, target, 0)) % chips
            entries += [(rep_index - offset // half_steps) % rep_size, offset % half_steps]
    entries += [(rep_index - d) % rep_size for d in range(rep_size)]
    table = [facts_of(piece) for pair in zip(own_pieces, other_pieces) for piece in pair]
    table = jnp.concatenate(table + [jnp.stack(entries).astype(jnp.int32)])

    slabs = [scaled]
    for step in range(1, chips // 2):
        slabs += [forward, backward]
        forward, backward = along_ring(forward, 1), along_ring(backward, -1)
    del backward

    slab_shape = jax.ShapeDtypeStruct((slab_rows, share_width), jnp.float32)
    term_shape = jax.ShapeDtypeStruct((width, share_width), jnp.bfloat16)
    def add_slabs(first_slab, slabs, sums):
        operands = own_pieces + other_pieces + slabs
        aliases = {1 + len(operands) + target: target for target in range(len(sums))}
        operands = operands + sums
        return pl.pallas_call(
            functools.partial(adding_kernel, plan, first_slab, len(slabs)),
            out_shape=(slab_shape, slab_shape),
            in_specs=[SMEM] + [VMEM] * len(operands),
            out_specs=(VMEM, VMEM),
            input_output_aliases=aliases,
            compiler_params=PARAMS,
            cost_estimate=COST,
            name="add_slabs",
        )(table, *operands)

    early = len(slabs) - 4
    sums = add_slabs(0, slabs[:early], [])
    for at in range(early, len(slabs), 2):
        sums = add_slabs(at, slabs[at : at + 2], list(sums))
    own_sums, other_sums, term = pl.pallas_call(
        functools.partial(last_kernel, plan, len(slabs)),
        out_shape=(slab_shape, slab_shape, term_shape),
        in_specs=[SMEM] + [VMEM] * (4 * rep_size + 3),
        out_specs=(VMEM,) * 3,
        compiler_params=PARAMS,
        cost_estimate=COST,
        name="last_slab",
    )(table, *own_pieces, *other_pieces, *own_features, *other_features, forward, *sums)

    def wide(values):
        return values.astype(jnp.float32)

    total = (wide(term) + wide(across_cores(term))).astype(jnp.bfloat16)
    own_sums = own_sums + across_cores(other_sums)
    aggregated = (own_sums * inverse_root[:, None]).astype(jnp.bfloat16)
    row_bits = [1 << bit for bit in range(rows_of_chips.bit_length() - 1)]
    first_bit, last_bit = row_bits[0], row_bits[-1]
    one = across(total, (first_bit, 1, 0), (first_bit, 0, 0))
    two = across(total, None, (0, 1, 0))
    part = wide(one) + wide(jnp.where(core == 0, total, two))
    total = part + across_cores(part)
    for bit in row_bits[1:-1]:
        total = total.astype(jnp.bfloat16)
        total = wide(total) + wide(across(total, (bit, 0, 0), (bit, 0, 0)))
    total, aggregated = lax.optimization_barrier((total, aggregated))
    total = total.astype(jnp.bfloat16)
    result = jnp.zeros((share_rows, width), jnp.float32)
    shares = []
    for d in range(rep_size):
        rows_to = ((rep_index + d) % rep_size) * share_rows
        part = lax.dynamic_slice_in_dim(aggregated, rows_to, share_rows, 0)
        if d:
            far = across(total, (last_bit, 0, 0), (last_bit, 0, d))
            both = along_rep(jnp.concatenate([part, total]), d)
            part, near = both[:share_rows], both[share_rows:]
            shares.append(wide(jnp.where(core == 0, total, near)) + wide(far))
        columns_at = ((rep_index - d) % rep_size) * share_width
        side = lax.dynamic_slice_in_dim(weight, columns_at, share_width, 1)
        result = result + lax.dot_general(
            part, side, (((1,), (1,)), ((), ())), preferred_element_type=jnp.float32
        )
    input_grad = result.astype(jnp.bfloat16)
    shares = jnp.stack(shares)
    others = across_cores(shares)
    own_share = jnp.where(core == 0, shares[0], others[0])
    other_shares = jnp.where(core == 0, others, shares)
    weight_grad = jnp.zeros((width, width), jnp.float32)
    for d in range(rep_size):
        columns_at = ((rep_index - d) % rep_size) * share_width
        share = other_shares[d - 1] if d else own_share
        weight_grad = lax.dynamic_update_slice_in_dim(weight_grad, share, columns_at, 1)
    weight_grad = weight_grad * (1.0 / math.sqrt(slab_rows * blk_size))
    return (input_grad, weight_grad)


def solution(mesh):
    return jax.shard_map(
        per_device,
        mesh=mesh,
        in_specs=(
            P(("blk", "rep"), None),
            P("blk", None),
            P(),
            P("blk", "rep", None, None, None),
            P("blk", "rep", None, None),
            P("blk", "rep"),
            P("blk"),
        ),
        out_specs=(P(("blk", "rep"), None), P()),
        check_vma=False,
    )
```

```python
import functools
import math

import jax
import jax.numpy as jnp
from jax import lax
from jax.experimental import pallas as pl
from jax.experimental.pallas import tpu as pltpu
from jax.sharding import PartitionSpec as P

CORES = 2
COLUMNS = 2


def device_of(row, column, core):
    return (row * COLUMNS + column) * CORES + core


def places(blk_size):
    rows = blk_size // (COLUMNS * CORES)
    return [(z, x, c) for z in range(rows) for x in range(COLUMNS) for c in range(CORES)]


def ring_order(rows):
    return [(z, 0) for z in range(rows)] + [(z, 1) for z in reversed(range(rows))]


def along_ring(block, distance):
    rows = lax.axis_size("blk") // (COLUMNS * CORES)
    order = ring_order(rows)
    route = []
    for place, (z, x) in enumerate(order):
        to_z, to_x = order[(place + distance) % len(order)]
        route += [(device_of(z, x, c), device_of(to_z, to_x, c)) for c in range(CORES)]
    return lax.ppermute(block, "blk", route)


def across(block, *moves):
    size = lax.axis_size("rep")
    route = []
    for z, x, c in places(lax.axis_size("blk")):
        if moves[c] is not None:
            rows, columns, reps = moves[c]
            start, end = device_of(z, x, c), device_of(z ^ rows, x ^ columns, c)
            route += [(start * size + r, end * size + (r + reps) % size) for r in range(size)]
    return lax.ppermute(block, ("blk", "rep"), route)


def across_cores(block):
    route = [
        (device_of(z, x, c), device_of(z, x, 1 - c)) for z, x, c in places(lax.axis_size("blk"))
    ]
    return lax.ppermute(block, "blk", route)


def along_rep(block, distance):
    size = lax.axis_size("rep")
    return lax.ppermute(block, "rep", [(i, (i + distance) % size) for i in range(size)])


def along_rep(block, distance):
    size = lax.axis_size("rep")
    return lax.ppermute(block, "rep", [(i, (i + distance) % size) for i in range(size)])


def across_columns_and_rep(block, distance):
    size = lax.axis_size("rep")
    route = [
        (device_of(z, x, c) * size + r, device_of(z, 1 - x, c) * size + (r + distance) % size)
        for z, x, c in places(lax.axis_size("blk"))
        for r in range(size)
    ]
    return lax.ppermute(block, ("blk", "rep"), route)


def from_all_reps(block):
    return [block] + [along_rep(block, d) for d in range(1, lax.axis_size("rep"))]


def add_pairs(plan, table_ref, first_slab, own_pieces, other_pieces, slabs, sums):
    bit_ids = lax.broadcasted_iota(jnp.int32, (16, 8, 128), 1)
    for slab_id, slab_ref in enumerate(slabs):
        for target, pieces in enumerate((own_pieces, other_pieces)):
            at = plan.facts_size + 2 * (2 * (first_slab + slab_id) + target)
            piece, pair = table_ref[at], table_ref[at + 1]
            base = ((piece * 2 + target) * plan.pairs + pair) * plan.facts
            live_count = table_ref[base]
            for slot in range(plan.slots):
                row_block = table_ref[base + 1 + slot]
                column_block = table_ref[base + 1 + plan.slots + slot]
                word_rows = pl.ds(pl.multiple_of(pair * plan.pair_rows + slot * 16, 16), 16)
                slot_words = jnp.zeros((16, 128), jnp.float32)
                for piece_id, piece_ref in enumerate(pieces):
                    chosen = jnp.logical_and(piece == piece_id, slot < live_count)
                    scale = jnp.where(chosen, 1.0, 0.0)
                    slot_words += piece_ref[word_rows, :].astype(jnp.float32) * scale
                slot_words = slot_words.astype(jnp.int32)
                bits = jnp.bitwise_and(jnp.right_shift(slot_words[:, None, :], bit_ids), 1)
                transposed = bits.reshape(128, 128).astype(jnp.float32).astype(jnp.bfloat16)
                rows = pl.ds(pl.multiple_of(row_block * 128, 128), 128)
                columns = pl.ds(pl.multiple_of(column_block * 128, 128), 128)
                sums[target][columns, :] += jnp.dot(
                    transposed, slab_ref[rows, :], preferred_element_type=jnp.float32
                )


def adding_kernel(plan, first_slab, slab_total, table_ref, *refs):
    own_pieces, other_pieces = refs[: plan.reps], refs[plan.reps : 2 * plan.reps]
    slabs, sums_in, sums = refs[2 * plan.reps :][:slab_total], refs[2 * plan.reps + slab_total : -2], refs[-2:]
    for target, sums_ref in enumerate(sums):
        sums_ref[...] = sums_in[target][...] if sums_in else jnp.zeros_like(sums_ref)
    add_pairs(plan, table_ref, first_slab, own_pieces, other_pieces, slabs, sums)


def last_kernel(plan, last_slab, table_ref, *refs):
    own_pieces, other_pieces = refs[: plan.reps], refs[plan.reps : 2 * plan.reps]
    own_features, other_features = refs[2 * plan.reps : 3 * plan.reps], refs[3 * plan.reps : 4 * plan.reps]
    slab_ref, own_in, other_in, own_ref, other_ref, term_ref, total_ref = refs[4 * plan.reps :]
    own_ref[...] = own_in[...]
    total_ref[...] = other_in[...]
    sums = (own_ref, total_ref)
    add_pairs(plan, table_ref, last_slab, own_pieces, other_pieces, [slab_ref], sums)
    other_ref[...] = total_ref[...].astype(other_ref.dtype)
    share = own_ref.shape[0] // plan.reps
    order_at = plan.facts_size + 4 * (last_slab + 1)
    term = jnp.zeros(term_ref.shape, jnp.float32)
    for sums_ref, pieces in zip(sums, (own_features, other_features)):
        for piece_id, piece_ref in enumerate(pieces):
            rows = pl.ds(pl.multiple_of(table_ref[order_at + piece_id] * share, share), share)
            part = sums_ref[rows, :].astype(jnp.bfloat16)
            term += jnp.dot(piece_ref[...], part, preferred_element_type=jnp.float32)
    term_ref[...] = term.astype(term_ref.dtype)


class Plan:
    def __init__(self, reps, slots, pairs):
        self.reps, self.slots, self.pairs = reps, slots, pairs
        self.pair_rows = slots * 16 + 16
        self.facts = 1 + 2 * slots
        self.facts_size = reps * 2 * pairs * self.facts


def scale_kernel(share_width, degrees_hbm, gradient_hbm, scaled_ref, degrees_ref, rows_ref, semaphores):
    start = pl.multiple_of(lax.axis_index("rep") * share_width, share_width)
    chunks = semaphores.shape[0] - 1
    chunk_rows = rows_ref.shape[0] // chunks
    degrees_copy = pltpu.make_async_copy(degrees_hbm, degrees_ref, semaphores.at[chunks])
    degrees_copy.start()
    copies = []
    for chunk in range(chunks):
        rows = pl.ds(chunk * chunk_rows, chunk_rows)
        copies.append(
            pltpu.make_async_copy(gradient_hbm.at[rows], rows_ref.at[rows], semaphores.at[chunk])
        )
        copies[-1].start()
    degrees_copy.wait()
    roots = lax.rsqrt(degrees_ref[...].astype(jnp.float32))
    for chunk in range(chunks):
        copies[chunk].wait()
        for at in range(chunk * chunk_rows, (chunk + 1) * chunk_rows, 128):
            row = at // 128
            by_row = jnp.broadcast_to(roots[row : row + 1, :], (128, 128)).T
            for column in range(0, share_width, 128):
                own = pl.ds(pl.multiple_of(start + column, 128), 128)
                part = rows_ref[at : at + 128, own].astype(jnp.float32) * by_row
                scaled_ref[at : at + 128, column : column + 128] = part.astype(scaled_ref.dtype)


def payload_kernel(plan, facts_ref, words_ref, features_ref, roots_ref, pairs_ref, turned_ref):
    word_rows = plan.slots * 16
    for step in range(2 * plan.pairs):
        start = ((step % 2) * plan.pairs + step // 2) * plan.pair_rows
        words = words_ref[step].astype(jnp.float32).astype(pairs_ref.dtype)
        pairs_ref[start : start + word_rows, :] = words
        facts = jnp.broadcast_to(facts_ref[step : step + 1, :].astype(jnp.float32), (16, 128))
        pairs_ref[start + word_rows : start + plan.pair_rows, :] = facts.astype(pairs_ref.dtype)
    for at in range(0, features_ref.shape[0], 128):
        part = features_ref[at : at + 128, :].astype(jnp.float32).T * roots_ref[:, at : at + 128]
        turned_ref[:, at : at + 128] = part.astype(turned_ref.dtype)


SMEM = pl.BlockSpec(memory_space=pltpu.SMEM)
VMEM = pl.BlockSpec(memory_space=pltpu.VMEM)
COST = pl.CostEstimate(flops=1, bytes_accessed=1, transcendentals=0)
PARAMS = pltpu.CompilerParams(vmem_limit_bytes=12 * 1024 * 1024)


def in_hbm(block):
    return pltpu.with_memory_space_constraint(block, pltpu.HBM)


def per_device(features, out_grad, weight, block_words, block_coords, block_counts, degrees):
    slab_rows, width = out_grad.shape
    rep_size = lax.axis_size("rep")
    blk_size = lax.axis_size("blk")
    chips = blk_size // CORES
    rows_of_chips = chips // COLUMNS
    rep_index = lax.axis_index("rep")
    blk_index = lax.axis_index("blk")
    core = blk_index % CORES
    chip = blk_index // CORES
    share_width = width // rep_size
    share_rows = slab_rows // rep_size
    slot_total = block_words.shape[2]
    half_steps = block_words.shape[1] // 2

    inverse_root = lax.rsqrt(degrees.astype(jnp.float32))
    if share_width % 128 == 0 and slab_rows % 1024 == 0:
        scaled = pl.pallas_call(
            functools.partial(scale_kernel, share_width),
            out_shape=pltpu.VMEM((slab_rows, share_width), jnp.bfloat16),
            in_specs=[pl.BlockSpec(memory_space=pltpu.HBM)] * 2,
            out_specs=VMEM,
            scratch_shapes=[
                pltpu.VMEM((slab_rows // 128, 128), jnp.int32),
                pltpu.VMEM((slab_rows, width), jnp.bfloat16),
                pltpu.SemaphoreType.DMA((5,)),
            ],
            compiler_params=PARAMS,
            name="scale",
        )(in_hbm(degrees.reshape(slab_rows // 128, 128)), in_hbm(out_grad))
    else:
        own_columns = lax.dynamic_slice_in_dim(out_grad, rep_index * share_width, share_width, 1)
        scaled = (own_columns.astype(jnp.float32) * inverse_root[:, None]).astype(jnp.bfloat16)

    forward, backward = along_ring(scaled, 1), along_ring(scaled, -1)

    block_words, features, _ = lax.optimization_barrier((block_words, features, scaled))
    plan = Plan(rep_size, slot_total, half_steps)
    facts = jnp.concatenate(
        [block_counts[0][:, None], block_coords[0].reshape(2 * half_steps, 2 * slot_total)], axis=1
    )
    facts = jnp.pad(facts, ((0, 0), (0, 128 - plan.facts)))
    words_rows = half_steps * plan.pair_rows
    share_root = lax.dynamic_slice_in_dim(inverse_root, rep_index * share_rows, share_rows, 0)
    pairs, turned = pl.pallas_call(
        functools.partial(payload_kernel, plan),
        out_shape=(
            jax.ShapeDtypeStruct((2 * words_rows, 128), jnp.bfloat16),
            jax.ShapeDtypeStruct((width, share_rows), jnp.bfloat16),
        ),
        in_specs=[VMEM] * 4,
        out_specs=(VMEM, VMEM),
        compiler_params=PARAMS,
        cost_estimate=COST,
        name="payload",
    )(facts, block_words[0].reshape(2 * half_steps, slot_total * 16, 128), features, share_root[None])
    both_pieces = from_all_reps(pairs)
    other_pieces = [across_cores(piece[words_rows:]) for piece in both_pieces]
    own_pieces = [piece[:words_rows] for piece in both_pieces]
    own_features = from_all_reps(turned)
    other_features = [across_cores(piece) for piece in own_features]

    def facts_of(piece):
        rows = piece[:words_rows].reshape(half_steps, plan.pair_rows, 128)[:, slot_total * 16]
        return rows[:, : plan.facts].astype(jnp.int32).reshape(-1)

    ring_row = chip // COLUMNS
    place = jnp.where(chip % COLUMNS == 0, ring_row, chips - 1 - ring_row)
    distances = [0]
    for step in range(1, chips // 2):
        distances += [-step, step]
    distances.append(chips // 2)
    entries = []
    for distance in distances:
        at = (place + distance) % chips
        source = jnp.where(at < rows_of_chips, at * COLUMNS, (chips - 1 - at) * COLUMNS + 1)
        for target in range(2):
            offset = (source - chip - jnp.where(core == 0, target, 0)) % chips
            entries += [(rep_index - offset // half_steps) % rep_size, offset % half_steps]
    entries += [(rep_index - d) % rep_size for d in range(rep_size)]
    table = [facts_of(piece) for pair in zip(own_pieces, other_pieces) for piece in pair]
    table = jnp.concatenate(table + [jnp.stack(entries).astype(jnp.int32)])

    slabs = [scaled]
    for step in range(1, chips // 2):
        slabs += [forward, backward]
        forward, backward = along_ring(forward, 1), along_ring(backward, -1)
    del backward

    slab_shape = jax.ShapeDtypeStruct((slab_rows, share_width), jnp.float32)
    sent_shape = jax.ShapeDtypeStruct((slab_rows, share_width), jnp.bfloat16)
    term_shape = jax.ShapeDtypeStruct((width, share_width), jnp.bfloat16)
    def add_slabs(first_slab, slabs, sums):
        operands = own_pieces + other_pieces + slabs
        aliases = {1 + len(operands) + target: target for target in range(len(sums))}
        operands = operands + sums
        return pl.pallas_call(
            functools.partial(adding_kernel, plan, first_slab, len(slabs)),
            out_shape=(slab_shape, slab_shape),
            in_specs=[SMEM] + [VMEM] * len(operands),
            out_specs=(VMEM, VMEM),
            input_output_aliases=aliases,
            compiler_params=PARAMS,
            cost_estimate=COST,
            name="add_slabs",
        )(table, *operands)

    early = len(slabs) - 4
    sums = add_slabs(0, slabs[:early], [])
    sums = add_slabs(early, slabs[early:-1], list(sums))
    sums = add_slabs(len(slabs) - 1, slabs[-1:], list(sums))
    own_sums, other_sums, term = pl.pallas_call(
        functools.partial(last_kernel, plan, len(slabs)),
        out_shape=(slab_shape, sent_shape, term_shape),
        in_specs=[SMEM] + [VMEM] * (4 * rep_size + 3),
        out_specs=(VMEM,) * 3,
        scratch_shapes=[pltpu.VMEM((slab_rows, share_width), jnp.float32)],
        compiler_params=PARAMS,
        cost_estimate=COST,
        name="last_slab",
    )(table, *own_pieces, *other_pieces, *own_features, *other_features, forward, *sums)

    def wide(values):
        return values.astype(jnp.float32)

    total = (wide(term) + wide(across_cores(term))).astype(jnp.bfloat16)
    own_sums = own_sums + wide(across_cores(other_sums))
    aggregated = (own_sums * inverse_root[:, None]).astype(jnp.bfloat16)
    row_bits = [1 << bit for bit in range(rows_of_chips.bit_length() - 1)]
    first_bit, last_bit = row_bits[0], row_bits[-1]
    one = across(total, (first_bit, 1, 0), (first_bit, 0, 0))
    two = across(total, None, (0, 1, 0))
    part = wide(one) + wide(jnp.where(core == 0, total, two))
    part, aggregated = lax.optimization_barrier((part, aggregated))
    total = part + across_cores(part)
    for bit in row_bits[1:-1]:
        total = total.astype(jnp.bfloat16)
        total = wide(total) + wide(across(total, (bit, 0, 0), (bit, 0, 0)))
    total = total.astype(jnp.bfloat16)
    result = jnp.zeros((share_rows, width), jnp.float32)
    shares = []
    for d in range(rep_size):
        rows_to = ((rep_index + d) % rep_size) * share_rows
        part = lax.dynamic_slice_in_dim(aggregated, rows_to, share_rows, 0)
        if d:
            far = across(total, (last_bit, 0, 0), (last_bit, 0, d))
            both = along_rep(jnp.concatenate([part, total]), d)
            part, near = both[:share_rows], both[share_rows:]
            shares.append(wide(jnp.where(core == 0, total, near)) + wide(far))
        columns_at = ((rep_index - d) % rep_size) * share_width
        side = lax.dynamic_slice_in_dim(weight, columns_at, share_width, 1)
        result = result + lax.dot_general(
            part, side, (((1,), (1,)), ((), ())), preferred_element_type=jnp.float32
        )
    input_grad = result.astype(jnp.bfloat16)
    shares = jnp.stack(shares)
    others = across_cores(shares)
    own_share = jnp.where(core == 0, shares[0], others[0])
    other_shares = jnp.where(core == 0, others, shares)
    weight_grad = jnp.zeros((width, width), jnp.float32)
    for d in range(rep_size):
        columns_at = ((rep_index - d) % rep_size) * share_width
        share = other_shares[d - 1] if d else own_share
        weight_grad = lax.dynamic_update_slice_in_dim(weight_grad, share, columns_at, 1)
    weight_grad = weight_grad * (1.0 / math.sqrt(slab_rows * blk_size))
    return (input_grad, weight_grad)


def solution(mesh):
    return jax.shard_map(
        per_device,
        mesh=mesh,
        in_specs=(
            P(("blk", "rep"), None),
            P("blk", None),
            P(),
            P("blk", "rep", None, None, None),
            P("blk", "rep", None, None),
            P("blk", "rep"),
            P("blk"),
        ),
        out_specs=(P(("blk", "rep"), None), P()),
        check_vma=False,
    )
```

```python
import functools
import math

import jax
import jax.numpy as jnp
from jax import lax
from jax.experimental import pallas as pl
from jax.experimental.pallas import tpu as pltpu
from jax.sharding import PartitionSpec as P

CORES = 2
COLUMNS = 2


def device_of(row, column, core):
    return (row * COLUMNS + column) * CORES + core


def places(blk_size):
    rows = blk_size // (COLUMNS * CORES)
    return [(z, x, c) for z in range(rows) for x in range(COLUMNS) for c in range(CORES)]


def ring_order(rows):
    return [(z, 0) for z in range(rows)] + [(z, 1) for z in reversed(range(rows))]


def along_ring(block, distance):
    rows = lax.axis_size("blk") // (COLUMNS * CORES)
    order = ring_order(rows)
    route = []
    for place, (z, x) in enumerate(order):
        to_z, to_x = order[(place + distance) % len(order)]
        route += [(device_of(z, x, c), device_of(to_z, to_x, c)) for c in range(CORES)]
    return lax.ppermute(block, "blk", route)


def across(block, *moves):
    size = lax.axis_size("rep")
    route = []
    for z, x, c in places(lax.axis_size("blk")):
        if moves[c] is not None:
            rows, columns, reps = moves[c]
            start, end = device_of(z, x, c), device_of(z ^ rows, x ^ columns, c)
            route += [(start * size + r, end * size + (r + reps) % size) for r in range(size)]
    return lax.ppermute(block, ("blk", "rep"), route)


def across_cores(block):
    route = [
        (device_of(z, x, c), device_of(z, x, 1 - c)) for z, x, c in places(lax.axis_size("blk"))
    ]
    return lax.ppermute(block, "blk", route)


def along_rep(block, distance):
    size = lax.axis_size("rep")
    return lax.ppermute(block, "rep", [(i, (i + distance) % size) for i in range(size)])


def along_rep(block, distance):
    size = lax.axis_size("rep")
    return lax.ppermute(block, "rep", [(i, (i + distance) % size) for i in range(size)])


def across_columns_and_rep(block, distance):
    size = lax.axis_size("rep")
    route = [
        (device_of(z, x, c) * size + r, device_of(z, 1 - x, c) * size + (r + distance) % size)
        for z, x, c in places(lax.axis_size("blk"))
        for r in range(size)
    ]
    return lax.ppermute(block, ("blk", "rep"), route)


def from_all_reps(block):
    return [block] + [along_rep(block, d) for d in range(1, lax.axis_size("rep"))]


def add_pairs(plan, table_ref, first_slab, own_pieces, other_pieces, slabs, sums):
    bit_ids = lax.broadcasted_iota(jnp.int32, (16, 8, 128), 1)
    for slab_id, slab_ref in enumerate(slabs):
        for target, pieces in enumerate((own_pieces, other_pieces)):
            at = plan.facts_size + 2 * (2 * (first_slab + slab_id) + target)
            piece, pair = table_ref[at], table_ref[at + 1]
            base = ((piece * 2 + target) * plan.pairs + pair) * plan.facts
            live_count = table_ref[base]
            for slot in range(plan.slots):
                row_block = table_ref[base + 1 + slot]
                column_block = table_ref[base + 1 + plan.slots + slot]
                word_rows = pl.ds(pl.multiple_of(pair * plan.pair_rows + slot * 16, 16), 16)
                slot_words = jnp.zeros((16, 128), jnp.float32)
                for piece_id, piece_ref in enumerate(pieces):
                    chosen = jnp.logical_and(piece == piece_id, slot < live_count)
                    scale = jnp.where(chosen, 1.0, 0.0)
                    slot_words += piece_ref[word_rows, :].astype(jnp.float32) * scale
                slot_words = slot_words.astype(jnp.int32)
                bits = jnp.bitwise_and(jnp.right_shift(slot_words[:, None, :], bit_ids), 1)
                transposed = bits.reshape(128, 128).astype(jnp.float32).astype(jnp.bfloat16)
                rows = pl.ds(pl.multiple_of(row_block * 128, 128), 128)
                columns = pl.ds(pl.multiple_of(column_block * 128, 128), 128)
                sums[target][columns, :] += jnp.dot(
                    transposed, slab_ref[rows, :], preferred_element_type=jnp.float32
                )


def adding_kernel(plan, first_slab, slab_total, table_ref, *refs):
    own_pieces, other_pieces = refs[: plan.reps], refs[plan.reps : 2 * plan.reps]
    slabs, sums_in, sums = refs[2 * plan.reps :][:slab_total], refs[2 * plan.reps + slab_total : -2], refs[-2:]
    for target, sums_ref in enumerate(sums):
        sums_ref[...] = sums_in[target][...] if sums_in else jnp.zeros_like(sums_ref)
    add_pairs(plan, table_ref, first_slab, own_pieces, other_pieces, slabs, sums)


def last_kernel(plan, last_slab, table_ref, *refs):
    own_pieces, other_pieces = refs[: plan.reps], refs[plan.reps : 2 * plan.reps]
    own_features, other_features = refs[2 * plan.reps : 3 * plan.reps], refs[3 * plan.reps : 4 * plan.reps]
    slab_ref, own_in, other_in, own_ref, other_ref, term_ref, total_ref = refs[4 * plan.reps :]
    own_ref[...] = own_in[...]
    total_ref[...] = other_in[...]
    sums = (own_ref, total_ref)
    add_pairs(plan, table_ref, last_slab, own_pieces, other_pieces, [slab_ref], sums)
    other_ref[...] = total_ref[...].astype(other_ref.dtype)
    share = own_ref.shape[0] // plan.reps
    order_at = plan.facts_size + 4 * (last_slab + 1)
    term = jnp.zeros(term_ref.shape, jnp.float32)
    for sums_ref, pieces in zip(sums, (own_features, other_features)):
        for piece_id, piece_ref in enumerate(pieces):
            rows = pl.ds(pl.multiple_of(table_ref[order_at + piece_id] * share, share), share)
            part = sums_ref[rows, :].astype(jnp.bfloat16)
            term += jnp.dot(piece_ref[...], part, preferred_element_type=jnp.float32)
    term_ref[...] = term.astype(term_ref.dtype)


class Plan:
    def __init__(self, reps, slots, pairs):
        self.reps, self.slots, self.pairs = reps, slots, pairs
        self.pair_rows = slots * 16 + 16
        self.facts = 1 + 2 * slots
        self.facts_size = reps * 2 * pairs * self.facts


def scale_kernel(share_width, degrees_hbm, gradient_hbm, scaled_ref, degrees_ref, rows_ref, semaphores):
    start = pl.multiple_of(lax.axis_index("rep") * share_width, share_width)
    chunks = semaphores.shape[0] - 1
    chunk_rows = rows_ref.shape[0] // chunks
    degrees_copy = pltpu.make_async_copy(degrees_hbm, degrees_ref, semaphores.at[chunks])
    degrees_copy.start()
    copies = []
    for chunk in range(chunks):
        rows = pl.ds(chunk * chunk_rows, chunk_rows)
        copies.append(
            pltpu.make_async_copy(gradient_hbm.at[rows], rows_ref.at[rows], semaphores.at[chunk])
        )
        copies[-1].start()
    degrees_copy.wait()
    roots = lax.rsqrt(degrees_ref[...].astype(jnp.float32))
    for chunk in range(chunks):
        copies[chunk].wait()
        for at in range(chunk * chunk_rows, (chunk + 1) * chunk_rows, 128):
            row = at // 128
            by_row = jnp.broadcast_to(roots[row : row + 1, :], (128, 128)).T
            for column in range(0, share_width, 128):
                own = pl.ds(pl.multiple_of(start + column, 128), 128)
                part = rows_ref[at : at + 128, own].astype(jnp.float32) * by_row
                scaled_ref[at : at + 128, column : column + 128] = part.astype(scaled_ref.dtype)


def payload_kernel(plan, facts_ref, words_ref, features_ref, roots_ref, pairs_ref, turned_ref):
    word_rows = plan.slots * 16
    for step in range(2 * plan.pairs):
        start = ((step % 2) * plan.pairs + step // 2) * plan.pair_rows
        words = words_ref[step].astype(jnp.float32).astype(pairs_ref.dtype)
        pairs_ref[start : start + word_rows, :] = words
        facts = jnp.broadcast_to(facts_ref[step : step + 1, :].astype(jnp.float32), (16, 128))
        pairs_ref[start + word_rows : start + plan.pair_rows, :] = facts.astype(pairs_ref.dtype)
    for at in range(0, features_ref.shape[0], 128):
        part = features_ref[at : at + 128, :].astype(jnp.float32).T * roots_ref[:, at : at + 128]
        turned_ref[:, at : at + 128] = part.astype(turned_ref.dtype)


SMEM = pl.BlockSpec(memory_space=pltpu.SMEM)
VMEM = pl.BlockSpec(memory_space=pltpu.VMEM)
COST = pl.CostEstimate(flops=1, bytes_accessed=1, transcendentals=0)
PARAMS = pltpu.CompilerParams(vmem_limit_bytes=12 * 1024 * 1024)


def in_hbm(block):
    return pltpu.with_memory_space_constraint(block, pltpu.HBM)


def per_device(features, out_grad, weight, block_words, block_coords, block_counts, degrees):
    slab_rows, width = out_grad.shape
    rep_size = lax.axis_size("rep")
    blk_size = lax.axis_size("blk")
    chips = blk_size // CORES
    rows_of_chips = chips // COLUMNS
    rep_index = lax.axis_index("rep")
    blk_index = lax.axis_index("blk")
    core = blk_index % CORES
    chip = blk_index // CORES
    share_width = width // rep_size
    share_rows = slab_rows // rep_size
    slot_total = block_words.shape[2]
    half_steps = block_words.shape[1] // 2

    inverse_root = lax.rsqrt(degrees.astype(jnp.float32))
    if share_width % 128 == 0 and slab_rows % 1024 == 0:
        scaled = pl.pallas_call(
            functools.partial(scale_kernel, share_width),
            out_shape=pltpu.VMEM((slab_rows, share_width), jnp.bfloat16),
            in_specs=[pl.BlockSpec(memory_space=pltpu.HBM)] * 2,
            out_specs=VMEM,
            scratch_shapes=[
                pltpu.VMEM((slab_rows // 128, 128), jnp.int32),
                pltpu.VMEM((slab_rows, width), jnp.bfloat16),
                pltpu.SemaphoreType.DMA((5,)),
            ],
            compiler_params=PARAMS,
            name="scale",
        )(in_hbm(degrees.reshape(slab_rows // 128, 128)), in_hbm(out_grad))
    else:
        own_columns = lax.dynamic_slice_in_dim(out_grad, rep_index * share_width, share_width, 1)
        scaled = (own_columns.astype(jnp.float32) * inverse_root[:, None]).astype(jnp.bfloat16)

    forward, backward = along_ring(scaled, 1), along_ring(scaled, -1)

    block_words, features, _ = lax.optimization_barrier((block_words, features, scaled))
    plan = Plan(rep_size, slot_total, half_steps)
    facts = jnp.concatenate(
        [block_counts[0][:, None], block_coords[0].reshape(2 * half_steps, 2 * slot_total)], axis=1
    )
    facts = jnp.pad(facts, ((0, 0), (0, 128 - plan.facts)))
    words_rows = half_steps * plan.pair_rows
    share_root = lax.dynamic_slice_in_dim(inverse_root, rep_index * share_rows, share_rows, 0)
    pairs, turned = pl.pallas_call(
        functools.partial(payload_kernel, plan),
        out_shape=(
            jax.ShapeDtypeStruct((2 * words_rows, 128), jnp.bfloat16),
            jax.ShapeDtypeStruct((width, share_rows), jnp.bfloat16),
        ),
        in_specs=[VMEM] * 4,
        out_specs=(VMEM, VMEM),
        compiler_params=PARAMS,
        cost_estimate=COST,
        name="payload",
    )(facts, block_words[0].reshape(2 * half_steps, slot_total * 16, 128), features, share_root[None])
    both_pieces = from_all_reps(pairs)
    other_pieces = [across_cores(piece[words_rows:]) for piece in both_pieces]
    own_pieces = [piece[:words_rows] for piece in both_pieces]
    own_features = from_all_reps(turned)
    other_features = [across_cores(piece) for piece in own_features]

    def facts_of(piece):
        rows = piece[:words_rows].reshape(half_steps, plan.pair_rows, 128)[:, slot_total * 16]
        return rows[:, : plan.facts].astype(jnp.int32).reshape(-1)

    ring_row = chip // COLUMNS
    place = jnp.where(chip % COLUMNS == 0, ring_row, chips - 1 - ring_row)
    distances = [0]
    for step in range(1, chips // 2):
        distances += [-step, step]
    distances.append(chips // 2)
    entries = []
    for distance in distances:
        at = (place + distance) % chips
        source = jnp.where(at < rows_of_chips, at * COLUMNS, (chips - 1 - at) * COLUMNS + 1)
        for target in range(2):
            offset = (source - chip - jnp.where(core == 0, target, 0)) % chips
            entries += [(rep_index - offset // half_steps) % rep_size, offset % half_steps]
    entries += [(rep_index - d) % rep_size for d in range(rep_size)]
    table = [facts_of(piece) for pair in zip(own_pieces, other_pieces) for piece in pair]
    table = jnp.concatenate(table + [jnp.stack(entries).astype(jnp.int32)])

    slabs = [scaled]
    for step in range(1, chips // 2):
        slabs += [forward, backward]
        forward, backward = along_ring(forward, 1), along_ring(backward, -1)
    del backward

    slab_shape = jax.ShapeDtypeStruct((slab_rows, share_width), jnp.float32)
    sent_shape = jax.ShapeDtypeStruct((slab_rows, share_width), jnp.bfloat16)
    term_shape = jax.ShapeDtypeStruct((width, share_width), jnp.bfloat16)
    def add_slabs(first_slab, slabs, sums):
        operands = own_pieces + other_pieces + slabs
        aliases = {1 + len(operands) + target: target for target in range(len(sums))}
        operands = operands + sums
        return pl.pallas_call(
            functools.partial(adding_kernel, plan, first_slab, len(slabs)),
            out_shape=(slab_shape, slab_shape),
            in_specs=[SMEM] + [VMEM] * len(operands),
            out_specs=(VMEM, VMEM),
            input_output_aliases=aliases,
            compiler_params=PARAMS,
            cost_estimate=COST,
            name="add_slabs",
        )(table, *operands)

    early = len(slabs) - 4
    sums = add_slabs(0, slabs[:early], [])
    sums = add_slabs(early, slabs[early:-1], list(sums))
    sums = add_slabs(len(slabs) - 1, slabs[-1:], list(sums))
    own_sums, other_sums, term = pl.pallas_call(
        functools.partial(last_kernel, plan, len(slabs)),
        out_shape=(slab_shape, sent_shape, term_shape),
        in_specs=[SMEM] + [VMEM] * (4 * rep_size + 3),
        out_specs=(VMEM,) * 3,
        scratch_shapes=[pltpu.VMEM((slab_rows, share_width), jnp.float32)],
        compiler_params=PARAMS,
        cost_estimate=COST,
        name="last_slab",
    )(table, *own_pieces, *other_pieces, *own_features, *other_features, forward, *sums)

    def wide(values):
        return values.astype(jnp.float32)

    total = (wide(term) + wide(across_cores(term))).astype(jnp.bfloat16)
    own_sums = own_sums + wide(across_cores(other_sums))
    aggregated = (own_sums * inverse_root[:, None]).astype(jnp.bfloat16)
    row_bits = [1 << bit for bit in range(rows_of_chips.bit_length() - 1)]
    one = across(total, (row_bits[0] | row_bits[1], 0, 0), (row_bits[1], 0, 0))
    two = across(total, None, (row_bits[0], 0, 0))
    part = wide(one) + wide(jnp.where(core == 0, total, two))
    part, aggregated = lax.optimization_barrier((part, aggregated))
    total = part + across_cores(part)
    for bit in row_bits[2:]:
        total = total.astype(jnp.bfloat16)
        total = wide(total) + wide(across(total, (bit, 0, 0), (bit, 0, 0)))
    total = total.astype(jnp.bfloat16)
    result = jnp.zeros((share_rows, width), jnp.float32)
    shares = []
    for d in range(rep_size):
        rows_to = ((rep_index + d) % rep_size) * share_rows
        part = lax.dynamic_slice_in_dim(aggregated, rows_to, share_rows, 0)
        if d:
            far = across(total, (0, 1, 0), (0, 1, d))
            part, near = along_rep(part, d), along_rep(total, d)
            shares.append(wide(jnp.where(core == 0, total, near)) + wide(far))
        columns_at = ((rep_index - d) % rep_size) * share_width
        side = lax.dynamic_slice_in_dim(weight, columns_at, share_width, 1)
        result = result + lax.dot_general(
            part, side, (((1,), (1,)), ((), ())), preferred_element_type=jnp.float32
        )
    input_grad = result.astype(jnp.bfloat16)
    shares = jnp.stack(shares)
    others = across_cores(shares)
    own_share = jnp.where(core == 0, shares[0], others[0])
    other_shares = jnp.where(core == 0, others, shares)
    weight_grad = jnp.zeros((width, width), jnp.float32)
    for d in range(rep_size):
        columns_at = ((rep_index - d) % rep_size) * share_width
        share = other_shares[d - 1] if d else own_share
        weight_grad = lax.dynamic_update_slice_in_dim(weight_grad, share, columns_at, 1)
    weight_grad = weight_grad * (1.0 / math.sqrt(slab_rows * blk_size))
    return (input_grad, weight_grad)


def solution(mesh):
    return jax.shard_map(
        per_device,
        mesh=mesh,
        in_specs=(
            P(("blk", "rep"), None),
            P("blk", None),
            P(),
            P("blk", "rep", None, None, None),
            P("blk", "rep", None, None),
            P("blk", "rep"),
            P("blk"),
        ),
        out_specs=(P(("blk", "rep"), None), P()),
        check_vma=False,
    )
```

```python
import functools
import math

import jax
import jax.numpy as jnp
from jax import lax
from jax.experimental import pallas as pl
from jax.experimental.pallas import tpu as pltpu
from jax.sharding import PartitionSpec as P

CORES = 2
COLUMNS = 2


def device_of(row, column, core):
    return (row * COLUMNS + column) * CORES + core


def places(blk_size):
    rows = blk_size // (COLUMNS * CORES)
    return [(z, x, c) for z in range(rows) for x in range(COLUMNS) for c in range(CORES)]


def ring_order(rows):
    return [(z, 0) for z in range(rows)] + [(z, 1) for z in reversed(range(rows))]


def along_ring(block, distance):
    rows = lax.axis_size("blk") // (COLUMNS * CORES)
    order = ring_order(rows)
    route = []
    for place, (z, x) in enumerate(order):
        to_z, to_x = order[(place + distance) % len(order)]
        route += [(device_of(z, x, c), device_of(to_z, to_x, c)) for c in range(CORES)]
    return lax.ppermute(block, "blk", route)


def across(block, *moves):
    size = lax.axis_size("rep")
    route = []
    for z, x, c in places(lax.axis_size("blk")):
        if moves[c] is not None:
            rows, columns, reps = moves[c]
            start, end = device_of(z, x, c), device_of(z ^ rows, x ^ columns, c)
            route += [(start * size + r, end * size + (r + reps) % size) for r in range(size)]
    return lax.ppermute(block, ("blk", "rep"), route)


def across_cores(block):
    route = [
        (device_of(z, x, c), device_of(z, x, 1 - c)) for z, x, c in places(lax.axis_size("blk"))
    ]
    return lax.ppermute(block, "blk", route)


def along_rep(block, distance):
    size = lax.axis_size("rep")
    return lax.ppermute(block, "rep", [(i, (i + distance) % size) for i in range(size)])


def along_rep(block, distance):
    size = lax.axis_size("rep")
    return lax.ppermute(block, "rep", [(i, (i + distance) % size) for i in range(size)])


def across_columns_and_rep(block, distance):
    size = lax.axis_size("rep")
    route = [
        (device_of(z, x, c) * size + r, device_of(z, 1 - x, c) * size + (r + distance) % size)
        for z, x, c in places(lax.axis_size("blk"))
        for r in range(size)
    ]
    return lax.ppermute(block, ("blk", "rep"), route)


def from_all_reps(block):
    return [block] + [along_rep(block, d) for d in range(1, lax.axis_size("rep"))]


def add_pairs(plan, table_ref, first_slab, own_pieces, other_pieces, slabs, sums):
    bit_ids = lax.broadcasted_iota(jnp.int32, (16, 8, 128), 1)
    for slab_id, slab_ref in enumerate(slabs):
        for target, pieces in enumerate((own_pieces, other_pieces)):
            at = plan.facts_size + 2 * (2 * (first_slab + slab_id) + target)
            piece, pair = table_ref[at], table_ref[at + 1]
            base = ((piece * 2 + target) * plan.pairs + pair) * plan.facts
            live_count = table_ref[base]
            for slot in range(plan.slots):
                row_block = table_ref[base + 1 + slot]
                column_block = table_ref[base + 1 + plan.slots + slot]
                word_rows = pl.ds(pl.multiple_of(pair * plan.pair_rows + slot * 16, 16), 16)
                slot_words = jnp.zeros((16, 128), jnp.float32)
                for piece_id, piece_ref in enumerate(pieces):
                    chosen = jnp.logical_and(piece == piece_id, slot < live_count)
                    scale = jnp.where(chosen, 1.0, 0.0)
                    slot_words += piece_ref[word_rows, :].astype(jnp.float32) * scale
                slot_words = slot_words.astype(jnp.int32)
                bits = jnp.bitwise_and(jnp.right_shift(slot_words[:, None, :], bit_ids), 1)
                transposed = bits.reshape(128, 128).astype(jnp.float32).astype(jnp.bfloat16)
                rows = pl.ds(pl.multiple_of(row_block * 128, 128), 128)
                columns = pl.ds(pl.multiple_of(column_block * 128, 128), 128)
                sums[target][columns, :] += jnp.dot(
                    transposed, slab_ref[rows, :], preferred_element_type=jnp.float32
                )


def adding_kernel(plan, first_slab, slab_total, table_ref, *refs):
    own_pieces, other_pieces = refs[: plan.reps], refs[plan.reps : 2 * plan.reps]
    slabs, sums_in, sums = refs[2 * plan.reps :][:slab_total], refs[2 * plan.reps + slab_total : -2], refs[-2:]
    for target, sums_ref in enumerate(sums):
        sums_ref[...] = sums_in[target][...] if sums_in else jnp.zeros_like(sums_ref)
    add_pairs(plan, table_ref, first_slab, own_pieces, other_pieces, slabs, sums)


def last_kernel(plan, last_slab, table_ref, *refs):
    own_pieces, other_pieces = refs[: plan.reps], refs[plan.reps : 2 * plan.reps]
    own_features, other_features = refs[2 * plan.reps : 3 * plan.reps], refs[3 * plan.reps : 4 * plan.reps]
    slab_ref, own_in, other_in, own_ref, other_ref, term_ref, total_ref = refs[4 * plan.reps :]
    own_ref[...] = own_in[...]
    total_ref[...] = other_in[...]
    sums = (own_ref, total_ref)
    add_pairs(plan, table_ref, last_slab, own_pieces, other_pieces, [slab_ref], sums)
    other_ref[...] = total_ref[...].astype(other_ref.dtype)
    share = own_ref.shape[0] // plan.reps
    order_at = plan.facts_size + 4 * (last_slab + 1)
    term = jnp.zeros(term_ref.shape, jnp.float32)
    for sums_ref, pieces in zip(sums, (own_features, other_features)):
        for piece_id, piece_ref in enumerate(pieces):
            rows = pl.ds(pl.multiple_of(table_ref[order_at + piece_id] * share, share), share)
            part = sums_ref[rows, :].astype(jnp.bfloat16)
            term += jnp.dot(piece_ref[...], part, preferred_element_type=jnp.float32)
    term_ref[...] = term.astype(term_ref.dtype)


class Plan:
    def __init__(self, reps, slots, pairs):
        self.reps, self.slots, self.pairs = reps, slots, pairs
        self.pair_rows = slots * 16 + 16
        self.facts = 1 + 2 * slots
        self.facts_size = reps * 2 * pairs * self.facts


def scale_kernel(share_width, degrees_hbm, gradient_hbm, scaled_ref, degrees_ref, rows_ref, semaphores):
    start = pl.multiple_of(lax.axis_index("rep") * share_width, share_width)
    chunks = semaphores.shape[0] - 1
    chunk_rows = rows_ref.shape[0] // chunks
    degrees_copy = pltpu.make_async_copy(degrees_hbm, degrees_ref, semaphores.at[chunks])
    degrees_copy.start()
    copies = []
    for chunk in range(chunks):
        rows = pl.ds(chunk * chunk_rows, chunk_rows)
        columns = gradient_hbm.at[rows, pl.ds(start, share_width)]
        copies.append(pltpu.make_async_copy(columns, rows_ref.at[rows], semaphores.at[chunk]))
        copies[-1].start()
    degrees_copy.wait()
    roots = lax.rsqrt(degrees_ref[...].astype(jnp.float32))
    for chunk in range(chunks):
        copies[chunk].wait()
        for at in range(chunk * chunk_rows, (chunk + 1) * chunk_rows, 128):
            row = at // 128
            by_row = jnp.broadcast_to(roots[row : row + 1, :], (128, 128)).T
            for column in range(0, share_width, 128):
                part = rows_ref[at : at + 128, column : column + 128].astype(jnp.float32) * by_row
                scaled_ref[at : at + 128, column : column + 128] = part.astype(scaled_ref.dtype)


def payload_kernel(plan, facts_ref, words_ref, features_ref, roots_ref, pairs_ref, turned_ref):
    word_rows = plan.slots * 16
    for step in range(2 * plan.pairs):
        start = ((step % 2) * plan.pairs + step // 2) * plan.pair_rows
        words = words_ref[step].astype(jnp.float32).astype(pairs_ref.dtype)
        pairs_ref[start : start + word_rows, :] = words
        facts = jnp.broadcast_to(facts_ref[step : step + 1, :].astype(jnp.float32), (16, 128))
        pairs_ref[start + word_rows : start + plan.pair_rows, :] = facts.astype(pairs_ref.dtype)
    for at in range(0, features_ref.shape[0], 128):
        part = features_ref[at : at + 128, :].astype(jnp.float32).T * roots_ref[:, at : at + 128]
        turned_ref[:, at : at + 128] = part.astype(turned_ref.dtype)


SMEM = pl.BlockSpec(memory_space=pltpu.SMEM)
VMEM = pl.BlockSpec(memory_space=pltpu.VMEM)
COST = pl.CostEstimate(flops=1, bytes_accessed=1, transcendentals=0)
PARAMS = pltpu.CompilerParams(vmem_limit_bytes=12 * 1024 * 1024)


def in_hbm(block):
    return pltpu.with_memory_space_constraint(block, pltpu.HBM)


def per_device(features, out_grad, weight, block_words, block_coords, block_counts, degrees):
    slab_rows, width = out_grad.shape
    rep_size = lax.axis_size("rep")
    blk_size = lax.axis_size("blk")
    chips = blk_size // CORES
    rows_of_chips = chips // COLUMNS
    rep_index = lax.axis_index("rep")
    blk_index = lax.axis_index("blk")
    core = blk_index % CORES
    chip = blk_index // CORES
    share_width = width // rep_size
    share_rows = slab_rows // rep_size
    slot_total = block_words.shape[2]
    half_steps = block_words.shape[1] // 2

    inverse_root = lax.rsqrt(degrees.astype(jnp.float32))
    if share_width % 128 == 0 and slab_rows % 1024 == 0:
        scaled = pl.pallas_call(
            functools.partial(scale_kernel, share_width),
            out_shape=pltpu.VMEM((slab_rows, share_width), jnp.bfloat16),
            in_specs=[pl.BlockSpec(memory_space=pltpu.HBM)] * 2,
            out_specs=VMEM,
            scratch_shapes=[
                pltpu.VMEM((slab_rows // 128, 128), jnp.int32),
                pltpu.VMEM((slab_rows, share_width), jnp.bfloat16),
                pltpu.SemaphoreType.DMA((3,)),
            ],
            compiler_params=PARAMS,
            name="scale",
        )(in_hbm(degrees.reshape(slab_rows // 128, 128)), in_hbm(out_grad))
    else:
        own_columns = lax.dynamic_slice_in_dim(out_grad, rep_index * share_width, share_width, 1)
        scaled = (own_columns.astype(jnp.float32) * inverse_root[:, None]).astype(jnp.bfloat16)

    forward, backward = along_ring(scaled, 1), along_ring(scaled, -1)

    block_words, features, _ = lax.optimization_barrier((block_words, features, scaled))
    plan = Plan(rep_size, slot_total, half_steps)
    facts = jnp.concatenate(
        [block_counts[0][:, None], block_coords[0].reshape(2 * half_steps, 2 * slot_total)], axis=1
    )
    facts = jnp.pad(facts, ((0, 0), (0, 128 - plan.facts)))
    words_rows = half_steps * plan.pair_rows
    share_root = lax.dynamic_slice_in_dim(inverse_root, rep_index * share_rows, share_rows, 0)
    pairs, turned = pl.pallas_call(
        functools.partial(payload_kernel, plan),
        out_shape=(
            jax.ShapeDtypeStruct((2 * words_rows, 128), jnp.bfloat16),
            jax.ShapeDtypeStruct((width, share_rows), jnp.bfloat16),
        ),
        in_specs=[VMEM] * 4,
        out_specs=(VMEM, VMEM),
        compiler_params=PARAMS,
        cost_estimate=COST,
        name="payload",
    )(facts, block_words[0].reshape(2 * half_steps, slot_total * 16, 128), features, share_root[None])
    both_pieces = from_all_reps(pairs)
    other_pieces = [across_cores(piece[words_rows:]) for piece in both_pieces]
    own_pieces = [piece[:words_rows] for piece in both_pieces]
    own_features = from_all_reps(turned)
    other_features = [across_cores(piece) for piece in own_features]

    def facts_of(piece):
        rows = piece[:words_rows].reshape(half_steps, plan.pair_rows, 128)[:, slot_total * 16]
        return rows[:, : plan.facts].astype(jnp.int32).reshape(-1)

    ring_row = chip // COLUMNS
    place = jnp.where(chip % COLUMNS == 0, ring_row, chips - 1 - ring_row)
    distances = [0]
    for step in range(1, chips // 2):
        distances += [-step, step]
    distances.append(chips // 2)
    entries = []
    for distance in distances:
        at = (place + distance) % chips
        source = jnp.where(at < rows_of_chips, at * COLUMNS, (chips - 1 - at) * COLUMNS + 1)
        for target in range(2):
            offset = (source - chip - jnp.where(core == 0, target, 0)) % chips
            entries += [(rep_index - offset // half_steps) % rep_size, offset % half_steps]
    entries += [(rep_index - d) % rep_size for d in range(rep_size)]
    table = [facts_of(piece) for pair in zip(own_pieces, other_pieces) for piece in pair]
    table = jnp.concatenate(table + [jnp.stack(entries).astype(jnp.int32)])

    slabs = [scaled]
    for step in range(1, chips // 2):
        slabs += [forward, backward]
        forward, backward = along_ring(forward, 1), along_ring(backward, -1)
    del backward

    slab_shape = jax.ShapeDtypeStruct((slab_rows, share_width), jnp.float32)
    sent_shape = jax.ShapeDtypeStruct((slab_rows, share_width), jnp.bfloat16)
    term_shape = jax.ShapeDtypeStruct((width, share_width), jnp.bfloat16)
    def add_slabs(first_slab, slabs, sums):
        operands = own_pieces + other_pieces + slabs
        aliases = {1 + len(operands) + target: target for target in range(len(sums))}
        operands = operands + sums
        return pl.pallas_call(
            functools.partial(adding_kernel, plan, first_slab, len(slabs)),
            out_shape=(slab_shape, slab_shape),
            in_specs=[SMEM] + [VMEM] * len(operands),
            out_specs=(VMEM, VMEM),
            input_output_aliases=aliases,
            compiler_params=PARAMS,
            cost_estimate=COST,
            name="add_slabs",
        )(table, *operands)

    early = len(slabs) - 4
    sums = add_slabs(0, slabs[:early], [])
    sums = add_slabs(early, slabs[early:-1], list(sums))
    sums = add_slabs(len(slabs) - 1, slabs[-1:], list(sums))
    own_sums, other_sums, term = pl.pallas_call(
        functools.partial(last_kernel, plan, len(slabs)),
        out_shape=(slab_shape, sent_shape, term_shape),
        in_specs=[SMEM] + [VMEM] * (4 * rep_size + 3),
        out_specs=(VMEM,) * 3,
        scratch_shapes=[pltpu.VMEM((slab_rows, share_width), jnp.float32)],
        compiler_params=PARAMS,
        cost_estimate=COST,
        name="last_slab",
    )(table, *own_pieces, *other_pieces, *own_features, *other_features, forward, *sums)

    def wide(values):
        return values.astype(jnp.float32)

    total = (wide(term) + wide(across_cores(term))).astype(jnp.bfloat16)
    own_sums = own_sums + wide(across_cores(other_sums))
    aggregated = (own_sums * inverse_root[:, None]).astype(jnp.bfloat16)
    row_bits = [1 << bit for bit in range(rows_of_chips.bit_length() - 1)]
    one = across(total, (row_bits[0] | row_bits[1], 0, 0), (row_bits[1], 0, 0))
    two = across(total, None, (row_bits[0], 0, 0))
    part = wide(one) + wide(jnp.where(core == 0, total, two))
    part, aggregated = lax.optimization_barrier((part, aggregated))
    total = part + across_cores(part)
    for bit in row_bits[2:]:
        total = total.astype(jnp.bfloat16)
        total = wide(total) + wide(across(total, (bit, 0, 0), (bit, 0, 0)))
    total = total.astype(jnp.bfloat16)
    result = jnp.zeros((share_rows, width), jnp.float32)
    shares = []
    for d in range(rep_size):
        rows_to = ((rep_index + d) % rep_size) * share_rows
        part = lax.dynamic_slice_in_dim(aggregated, rows_to, share_rows, 0)
        if d:
            far = across(total, (0, 1, 0), (0, 1, d))
            part, near = along_rep(part, d), along_rep(total, d)
            shares.append(wide(jnp.where(core == 0, total, near)) + wide(far))
        columns_at = ((rep_index - d) % rep_size) * share_width
        side = lax.dynamic_slice_in_dim(weight, columns_at, share_width, 1)
        result = result + lax.dot_general(
            part, side, (((1,), (1,)), ((), ())), preferred_element_type=jnp.float32
        )
    input_grad = result.astype(jnp.bfloat16)
    shares = jnp.stack(shares)
    shares, input_grad = lax.optimization_barrier((shares, input_grad))
    others = across_cores(shares)
    own_share = jnp.where(core == 0, shares[0], others[0])
    other_shares = jnp.where(core == 0, others, shares)
    weight_grad = jnp.zeros((width, width), jnp.float32)
    for d in range(rep_size):
        columns_at = ((rep_index - d) % rep_size) * share_width
        share = other_shares[d - 1] if d else own_share
        weight_grad = lax.dynamic_update_slice_in_dim(weight_grad, share, columns_at, 1)
    weight_grad = weight_grad * (1.0 / math.sqrt(slab_rows * blk_size))
    return (input_grad, weight_grad)


def solution(mesh):
    return jax.shard_map(
        per_device,
        mesh=mesh,
        in_specs=(
            P(("blk", "rep"), None),
            P("blk", None),
            P(),
            P("blk", "rep", None, None, None),
            P("blk", "rep", None, None),
            P("blk", "rep"),
            P("blk"),
        ),
        out_specs=(P(("blk", "rep"), None), P()),
        check_vma=False,
    )
```

```python
import functools
import math

import jax
import jax.numpy as jnp
from jax import lax
from jax.experimental import pallas as pl
from jax.experimental.pallas import tpu as pltpu
from jax.sharding import PartitionSpec as P

CORES = 2
COLUMNS = 2


def device_of(row, column, core):
    return (row * COLUMNS + column) * CORES + core


def places(blk_size):
    rows = blk_size // (COLUMNS * CORES)
    return [(z, x, c) for z in range(rows) for x in range(COLUMNS) for c in range(CORES)]


def ring_order(rows):
    return [(z, 0) for z in range(rows)] + [(z, 1) for z in reversed(range(rows))]


def along_ring(block, distance):
    rows = lax.axis_size("blk") // (COLUMNS * CORES)
    order = ring_order(rows)
    route = []
    for place, (z, x) in enumerate(order):
        to_z, to_x = order[(place + distance) % len(order)]
        route += [(device_of(z, x, c), device_of(to_z, to_x, c)) for c in range(CORES)]
    return lax.ppermute(block, "blk", route)


def across(block, *moves):
    size = lax.axis_size("rep")
    route = []
    for z, x, c in places(lax.axis_size("blk")):
        if moves[c] is not None:
            rows, columns, reps = moves[c]
            start, end = device_of(z, x, c), device_of(z ^ rows, x ^ columns, c)
            route += [(start * size + r, end * size + (r + reps) % size) for r in range(size)]
    return lax.ppermute(block, ("blk", "rep"), route)


def across_cores(block):
    route = [
        (device_of(z, x, c), device_of(z, x, 1 - c)) for z, x, c in places(lax.axis_size("blk"))
    ]
    return lax.ppermute(block, "blk", route)


def along_rep(block, distance):
    size = lax.axis_size("rep")
    return lax.ppermute(block, "rep", [(i, (i + distance) % size) for i in range(size)])


def from_all_reps(block):
    return [block] + [along_rep(block, d) for d in range(1, lax.axis_size("rep"))]


def add_pairs(plan, table_ref, first_slab, own_pieces, other_pieces, slabs, sums):
    bit_ids = lax.broadcasted_iota(jnp.int32, (16, 8, 128), 1)
    for slab_id, slab_ref in enumerate(slabs):
        for target, pieces in enumerate((own_pieces, other_pieces)):
            at = plan.facts_size + 2 * (2 * (first_slab + slab_id) + target)
            piece, pair = table_ref[at], table_ref[at + 1]
            base = ((piece * 2 + target) * plan.pairs + pair) * plan.facts
            live_count = table_ref[base]
            for slot in range(plan.slots):
                row_block = table_ref[base + 1 + slot]
                column_block = table_ref[base + 1 + plan.slots + slot]
                word_rows = pl.ds(pl.multiple_of(pair * plan.pair_rows + slot * 16, 16), 16)
                slot_words = jnp.zeros((16, 128), jnp.float32)
                for piece_id, piece_ref in enumerate(pieces):
                    chosen = jnp.logical_and(piece == piece_id, slot < live_count)
                    scale = jnp.where(chosen, 1.0, 0.0)
                    slot_words += piece_ref[word_rows, :].astype(jnp.float32) * scale
                slot_words = slot_words.astype(jnp.int32)
                bits = jnp.bitwise_and(jnp.right_shift(slot_words[:, None, :], bit_ids), 1)
                transposed = bits.reshape(128, 128).astype(jnp.float32).astype(jnp.bfloat16)
                rows = pl.ds(pl.multiple_of(row_block * 128, 128), 128)
                columns = pl.ds(pl.multiple_of(column_block * 128, 128), 128)
                sums[target][columns, :] += jnp.dot(
                    transposed, slab_ref[rows, :], preferred_element_type=jnp.float32
                )


def adding_kernel(plan, first_slab, slab_total, table_ref, *refs):
    own_pieces, other_pieces = refs[: plan.reps], refs[plan.reps : 2 * plan.reps]
    slabs, sums_in, sums = refs[2 * plan.reps :][:slab_total], refs[2 * plan.reps + slab_total : -2], refs[-2:]
    for target, sums_ref in enumerate(sums):
        sums_ref[...] = sums_in[target][...] if sums_in else jnp.zeros_like(sums_ref)
    add_pairs(plan, table_ref, first_slab, own_pieces, other_pieces, slabs, sums)


def last_kernel(plan, last_slab, table_ref, *refs):
    own_pieces, other_pieces = refs[: plan.reps], refs[plan.reps : 2 * plan.reps]
    own_features, other_features = refs[2 * plan.reps : 3 * plan.reps], refs[3 * plan.reps : 4 * plan.reps]
    slab_ref, own_in, other_in, own_ref, other_ref, term_ref, total_ref = refs[4 * plan.reps :]
    own_ref[...] = own_in[...]
    total_ref[...] = other_in[...]
    sums = (own_ref, total_ref)
    add_pairs(plan, table_ref, last_slab, own_pieces, other_pieces, [slab_ref], sums)
    other_ref[...] = total_ref[...].astype(other_ref.dtype)
    share = own_ref.shape[0] // plan.reps
    order_at = plan.facts_size + 4 * (last_slab + 1)
    term = jnp.zeros(term_ref.shape, jnp.float32)
    for sums_ref, pieces in zip(sums, (own_features, other_features)):
        for piece_id, piece_ref in enumerate(pieces):
            rows = pl.ds(pl.multiple_of(table_ref[order_at + piece_id] * share, share), share)
            part = sums_ref[rows, :].astype(jnp.bfloat16)
            term += jnp.dot(piece_ref[...], part, preferred_element_type=jnp.float32)
    term_ref[...] = term.astype(term_ref.dtype)


class Plan:
    def __init__(self, reps, slots, pairs):
        self.reps, self.slots, self.pairs = reps, slots, pairs
        self.pair_rows = slots * 16 + 16
        self.facts = 1 + 2 * slots
        self.facts_size = reps * 2 * pairs * self.facts


def scale_kernel(share_width, degrees_hbm, gradient_hbm, scaled_ref, degrees_ref, rows_ref, semaphores):
    start = pl.multiple_of(lax.axis_index("rep") * share_width, share_width)
    chunks = semaphores.shape[0] - 1
    chunk_rows = rows_ref.shape[0] // chunks
    degrees_copy = pltpu.make_async_copy(degrees_hbm, degrees_ref, semaphores.at[chunks])
    degrees_copy.start()
    copies = []
    for chunk in range(chunks):
        rows = pl.ds(chunk * chunk_rows, chunk_rows)
        columns = gradient_hbm.at[rows, pl.ds(start, share_width)]
        copies.append(pltpu.make_async_copy(columns, rows_ref.at[rows], semaphores.at[chunk]))
        copies[-1].start()
    degrees_copy.wait()
    roots = lax.rsqrt(degrees_ref[...].astype(jnp.float32))
    for chunk in range(chunks):
        copies[chunk].wait()
        for at in range(chunk * chunk_rows, (chunk + 1) * chunk_rows, 128):
            row = at // 128
            by_row = jnp.broadcast_to(roots[row : row + 1, :], (128, 128)).T
            for column in range(0, share_width, 128):
                part = rows_ref[at : at + 128, column : column + 128].astype(jnp.float32) * by_row
                scaled_ref[at : at + 128, column : column + 128] = part.astype(scaled_ref.dtype)


def payload_kernel(plan, facts_ref, words_ref, features_ref, roots_ref, pairs_ref, turned_ref):
    word_rows = plan.slots * 16
    for step in range(2 * plan.pairs):
        start = ((step % 2) * plan.pairs + step // 2) * plan.pair_rows
        words = words_ref[step].astype(jnp.float32).astype(pairs_ref.dtype)
        pairs_ref[start : start + word_rows, :] = words
        facts = jnp.broadcast_to(facts_ref[step : step + 1, :].astype(jnp.float32), (16, 128))
        pairs_ref[start + word_rows : start + plan.pair_rows, :] = facts.astype(pairs_ref.dtype)
    for at in range(0, features_ref.shape[0], 128):
        part = features_ref[at : at + 128, :].astype(jnp.float32).T * roots_ref[:, at : at + 128]
        turned_ref[:, at : at + 128] = part.astype(turned_ref.dtype)


SMEM = pl.BlockSpec(memory_space=pltpu.SMEM)
VMEM = pl.BlockSpec(memory_space=pltpu.VMEM)
COST = pl.CostEstimate(flops=1, bytes_accessed=1, transcendentals=0)
PARAMS = pltpu.CompilerParams(vmem_limit_bytes=12 * 1024 * 1024)


def in_hbm(block):
    return pltpu.with_memory_space_constraint(block, pltpu.HBM)


def per_device(features, out_grad, weight, block_words, block_coords, block_counts, degrees):
    slab_rows, width = out_grad.shape
    rep_size = lax.axis_size("rep")
    blk_size = lax.axis_size("blk")
    chips = blk_size // CORES
    rows_of_chips = chips // COLUMNS
    rep_index = lax.axis_index("rep")
    blk_index = lax.axis_index("blk")
    core = blk_index % CORES
    chip = blk_index // CORES
    share_width = width // rep_size
    share_rows = slab_rows // rep_size
    slot_total = block_words.shape[2]
    half_steps = block_words.shape[1] // 2

    inverse_root = lax.rsqrt(degrees.astype(jnp.float32))
    if share_width % 128 == 0 and slab_rows % 1024 == 0:
        scaled = pl.pallas_call(
            functools.partial(scale_kernel, share_width),
            out_shape=pltpu.VMEM((slab_rows, share_width), jnp.bfloat16),
            in_specs=[pl.BlockSpec(memory_space=pltpu.HBM)] * 2,
            out_specs=VMEM,
            scratch_shapes=[
                pltpu.VMEM((slab_rows // 128, 128), jnp.int32),
                pltpu.VMEM((slab_rows, share_width), jnp.bfloat16),
                pltpu.SemaphoreType.DMA((3,)),
            ],
            compiler_params=PARAMS,
            name="scale",
        )(in_hbm(degrees.reshape(slab_rows // 128, 128)), in_hbm(out_grad))
    else:
        own_columns = lax.dynamic_slice_in_dim(out_grad, rep_index * share_width, share_width, 1)
        scaled = (own_columns.astype(jnp.float32) * inverse_root[:, None]).astype(jnp.bfloat16)

    forward, backward = along_ring(scaled, 1), along_ring(scaled, -1)

    block_words, features, _ = lax.optimization_barrier((block_words, features, scaled))
    plan = Plan(rep_size, slot_total, half_steps)
    facts = jnp.concatenate(
        [block_counts[0][:, None], block_coords[0].reshape(2 * half_steps, 2 * slot_total)], axis=1
    )
    facts = jnp.pad(facts, ((0, 0), (0, 128 - plan.facts)))
    words_rows = half_steps * plan.pair_rows
    share_root = lax.dynamic_slice_in_dim(inverse_root, rep_index * share_rows, share_rows, 0)
    pairs, turned = pl.pallas_call(
        functools.partial(payload_kernel, plan),
        out_shape=(
            jax.ShapeDtypeStruct((2 * words_rows, 128), jnp.bfloat16),
            jax.ShapeDtypeStruct((width, share_rows), jnp.bfloat16),
        ),
        in_specs=[VMEM] * 4,
        out_specs=(VMEM, VMEM),
        compiler_params=PARAMS,
        cost_estimate=COST,
        name="payload",
    )(facts, block_words[0].reshape(2 * half_steps, slot_total * 16, 128), features, share_root[None])
    both_pieces = from_all_reps(pairs)
    other_pieces = [across_cores(piece[words_rows:]) for piece in both_pieces]
    own_pieces = [piece[:words_rows] for piece in both_pieces]
    own_features = from_all_reps(turned)
    other_features = [across_cores(piece) for piece in own_features]

    def facts_of(piece):
        rows = piece[:words_rows].reshape(half_steps, plan.pair_rows, 128)[:, slot_total * 16]
        return rows[:, : plan.facts].astype(jnp.int32).reshape(-1)

    ring_row = chip // COLUMNS
    place = jnp.where(chip % COLUMNS == 0, ring_row, chips - 1 - ring_row)
    distances = [0]
    for step in range(1, chips // 2):
        distances += [-step, step]
    distances.append(chips // 2)
    entries = []
    for distance in distances:
        at = (place + distance) % chips
        source = jnp.where(at < rows_of_chips, at * COLUMNS, (chips - 1 - at) * COLUMNS + 1)
        for target in range(2):
            offset = (source - chip - jnp.where(core == 0, target, 0)) % chips
            entries += [(rep_index - offset // half_steps) % rep_size, offset % half_steps]
    entries += [(rep_index - d) % rep_size for d in range(rep_size)]
    table = [facts_of(piece) for pair in zip(own_pieces, other_pieces) for piece in pair]
    table = jnp.concatenate(table + [jnp.stack(entries).astype(jnp.int32)])

    slabs = [scaled]
    for step in range(1, chips // 2):
        slabs += [forward, backward]
        forward, backward = along_ring(forward, 1), along_ring(backward, -1)
    del backward

    slab_shape = jax.ShapeDtypeStruct((slab_rows, share_width), jnp.float32)
    sent_shape = jax.ShapeDtypeStruct((slab_rows, share_width), jnp.bfloat16)
    term_shape = jax.ShapeDtypeStruct((width, share_width), jnp.bfloat16)

    def add_slabs(first_slab, slabs, sums):
        operands = own_pieces + other_pieces + slabs
        aliases = {1 + len(operands) + target: target for target in range(len(sums))}
        operands = operands + sums
        return pl.pallas_call(
            functools.partial(adding_kernel, plan, first_slab, len(slabs)),
            out_shape=(slab_shape, slab_shape),
            in_specs=[SMEM] + [VMEM] * len(operands),
            out_specs=(VMEM, VMEM),
            input_output_aliases=aliases,
            compiler_params=PARAMS,
            cost_estimate=COST,
            name="add_slabs",
        )(table, *operands)

    early = len(slabs) - 4
    sums = add_slabs(0, slabs[:early], [])
    sums = add_slabs(early, slabs[early:-1], list(sums))
    sums = add_slabs(len(slabs) - 1, slabs[-1:], list(sums))
    own_sums, other_sums, term = pl.pallas_call(
        functools.partial(last_kernel, plan, len(slabs)),
        out_shape=(slab_shape, sent_shape, term_shape),
        in_specs=[SMEM] + [VMEM] * (4 * rep_size + 3),
        out_specs=(VMEM,) * 3,
        scratch_shapes=[pltpu.VMEM((slab_rows, share_width), jnp.float32)],
        compiler_params=PARAMS,
        cost_estimate=COST,
        name="last_slab",
    )(table, *own_pieces, *other_pieces, *own_features, *other_features, forward, *sums)

    def wide(values):
        return values.astype(jnp.float32)

    total = (wide(term) + wide(across_cores(term))).astype(jnp.bfloat16)
    own_sums = own_sums + wide(across_cores(other_sums))
    aggregated = (own_sums * inverse_root[:, None]).astype(jnp.bfloat16)
    row_bits = [1 << bit for bit in range(rows_of_chips.bit_length() - 1)]
    one = across(total, (row_bits[0] | row_bits[1], 0, 0), (row_bits[1], 0, 0))
    two = across(total, None, (row_bits[0], 0, 0))
    part = wide(one) + wide(jnp.where(core == 0, total, two))
    part, aggregated = lax.optimization_barrier((part, aggregated))
    total = part + across_cores(part)
    for bit in row_bits[2:]:
        total = total.astype(jnp.bfloat16)
        total = wide(total) + wide(across(total, (bit, 0, 0), (bit, 0, 0)))
    total = total.astype(jnp.bfloat16)
    result = jnp.zeros((share_rows, width), jnp.float32)
    shares = []
    for d in range(rep_size):
        rows_to = ((rep_index + d) % rep_size) * share_rows
        part = lax.dynamic_slice_in_dim(aggregated, rows_to, share_rows, 0)
        if d:
            far = across(total, (0, 1, 0), (0, 1, d))
            part, near = along_rep(part, d), along_rep(total, d)
            shares.append(wide(jnp.where(core == 0, total, near)) + wide(far))
        columns_at = ((rep_index - d) % rep_size) * share_width
        side = lax.dynamic_slice_in_dim(weight, columns_at, share_width, 1)
        result = result + lax.dot_general(
            part, side, (((1,), (1,)), ((), ())), preferred_element_type=jnp.float32
        )
    input_grad = result.astype(jnp.bfloat16)
    shares = jnp.stack(shares)
    shares, input_grad = lax.optimization_barrier((shares, input_grad))
    others = across_cores(shares)
    own_share = jnp.where(core == 0, shares[0], others[0])
    other_shares = jnp.where(core == 0, others, shares)
    weight_grad = jnp.zeros((width, width), jnp.float32)
    for d in range(rep_size):
        columns_at = ((rep_index - d) % rep_size) * share_width
        share = other_shares[d - 1] if d else own_share
        weight_grad = lax.dynamic_update_slice_in_dim(weight_grad, share, columns_at, 1)
    weight_grad = weight_grad * (1.0 / math.sqrt(slab_rows * blk_size))
    return (input_grad, weight_grad)


def solution(mesh):
    return jax.shard_map(
        per_device,
        mesh=mesh,
        in_specs=(
            P(("blk", "rep"), None),
            P("blk", None),
            P(),
            P("blk", "rep", None, None, None),
            P("blk", "rep", None, None),
            P("blk", "rep"),
            P("blk"),
        ),
        out_specs=(P(("blk", "rep"), None), P()),
        check_vma=False,
    )
```

```python
import functools
import math

import jax
import jax.numpy as jnp
from jax import lax
from jax.experimental import pallas as pl
from jax.experimental.pallas import tpu as pltpu
from jax.sharding import PartitionSpec as P

CORES = 2
COLUMNS = 2


def device_of(row, column, core):
    return (row * COLUMNS + column) * CORES + core


def places(blk_size):
    rows = blk_size // (COLUMNS * CORES)
    return [(z, x, c) for z in range(rows) for x in range(COLUMNS) for c in range(CORES)]


def ring_order(rows):
    return [(z, 0) for z in range(rows)] + [(z, 1) for z in reversed(range(rows))]


def along_ring(block, distance):
    rows = lax.axis_size("blk") // (COLUMNS * CORES)
    order = ring_order(rows)
    route = []
    for place, (z, x) in enumerate(order):
        to_z, to_x = order[(place + distance) % len(order)]
        route += [(device_of(z, x, c), device_of(to_z, to_x, c)) for c in range(CORES)]
    return lax.ppermute(block, "blk", route)


def across(block, *moves):
    size = lax.axis_size("rep")
    route = []
    for z, x, c in places(lax.axis_size("blk")):
        if moves[c] is not None:
            rows, columns, reps = moves[c]
            start, end = device_of(z, x, c), device_of(z ^ rows, x ^ columns, c)
            route += [(start * size + r, end * size + (r + reps) % size) for r in range(size)]
    return lax.ppermute(block, ("blk", "rep"), route)


def across_cores(block):
    route = [
        (device_of(z, x, c), device_of(z, x, 1 - c)) for z, x, c in places(lax.axis_size("blk"))
    ]
    return lax.ppermute(block, "blk", route)


def along_rep(block, distance):
    size = lax.axis_size("rep")
    return lax.ppermute(block, "rep", [(i, (i + distance) % size) for i in range(size)])


def from_all_reps(block):
    return [block] + [along_rep(block, d) for d in range(1, lax.axis_size("rep"))]


def add_pairs(plan, table_ref, first_slab, own_pieces, other_pieces, slabs, sums):
    bit_ids = lax.broadcasted_iota(jnp.int32, (16, 8, 128), 1)
    for slab_id, slab_ref in enumerate(slabs):
        for target, pieces in enumerate((own_pieces, other_pieces)):
            at = plan.facts_size + 2 * (2 * (first_slab + slab_id) + target)
            piece, pair = table_ref[at], table_ref[at + 1]
            base = ((piece * 2 + target) * plan.pairs + pair) * plan.facts
            live_count = table_ref[base]
            for slot in range(plan.slots):
                row_block = table_ref[base + 1 + slot]
                column_block = table_ref[base + 1 + plan.slots + slot]
                word_rows = pl.ds(pl.multiple_of(pair * plan.pair_rows + slot * 16, 16), 16)
                slot_words = jnp.zeros((16, 128), jnp.float32)
                for piece_id, piece_ref in enumerate(pieces):
                    chosen = jnp.logical_and(piece == piece_id, slot < live_count)
                    scale = jnp.where(chosen, 1.0, 0.0)
                    slot_words += piece_ref[word_rows, :].astype(jnp.float32) * scale
                slot_words = slot_words.astype(jnp.int32)
                bits = jnp.bitwise_and(jnp.right_shift(slot_words[:, None, :], bit_ids), 1)
                transposed = bits.reshape(128, 128).astype(jnp.float32).astype(jnp.bfloat16)
                rows = pl.ds(pl.multiple_of(row_block * 128, 128), 128)
                columns = pl.ds(pl.multiple_of(column_block * 128, 128), 128)
                sums[target][columns, :] += jnp.dot(
                    transposed, slab_ref[rows, :], preferred_element_type=jnp.float32
                )


def adding_kernel(plan, first_slab, slab_total, table_ref, *refs):
    own_pieces, other_pieces = refs[: plan.reps], refs[plan.reps : 2 * plan.reps]
    slabs, sums_in, sums = refs[2 * plan.reps :][:slab_total], refs[2 * plan.reps + slab_total : -2], refs[-2:]
    for target, sums_ref in enumerate(sums):
        sums_ref[...] = sums_in[target][...] if sums_in else jnp.zeros_like(sums_ref)
    add_pairs(plan, table_ref, first_slab, own_pieces, other_pieces, slabs, sums)


def last_kernel(plan, last_slab, table_ref, *refs):
    own_pieces, other_pieces = refs[: plan.reps], refs[plan.reps : 2 * plan.reps]
    own_features, other_features = refs[2 * plan.reps : 3 * plan.reps], refs[3 * plan.reps : 4 * plan.reps]
    slab_ref, own_in, other_in, own_ref, other_ref, term_ref, total_ref = refs[4 * plan.reps :]
    own_ref[...] = own_in[...]
    total_ref[...] = other_in[...]
    sums = (own_ref, total_ref)
    add_pairs(plan, table_ref, last_slab, own_pieces, other_pieces, [slab_ref], sums)
    other_ref[...] = total_ref[...].astype(other_ref.dtype)
    share = own_ref.shape[0] // plan.reps
    order_at = plan.facts_size + 4 * (last_slab + 1)
    term = jnp.zeros(term_ref.shape, jnp.float32)
    for sums_ref, pieces in zip(sums, (own_features, other_features)):
        for piece_id, piece_ref in enumerate(pieces):
            rows = pl.ds(pl.multiple_of(table_ref[order_at + piece_id] * share, share), share)
            part = sums_ref[rows, :].astype(jnp.bfloat16)
            term += jnp.dot(piece_ref[...], part, preferred_element_type=jnp.float32)
    term_ref[...] = term.astype(term_ref.dtype)


class Plan:
    def __init__(self, reps, slots, pairs):
        self.reps, self.slots, self.pairs = reps, slots, pairs
        self.pair_rows = slots * 16 + 16
        self.facts = 1 + 2 * slots
        self.facts_size = reps * 2 * pairs * self.facts


def scale_kernel(share_width, degrees_hbm, gradient_hbm, scaled_ref, degrees_ref, rows_ref, semaphores):
    start = pl.multiple_of(lax.axis_index("rep") * share_width, share_width)
    chunks = semaphores.shape[0] - 1
    chunk_rows = rows_ref.shape[0] // chunks
    degrees_copy = pltpu.make_async_copy(degrees_hbm, degrees_ref, semaphores.at[chunks])
    degrees_copy.start()
    copies = []
    for chunk in range(chunks):
        rows = pl.ds(chunk * chunk_rows, chunk_rows)
        columns = gradient_hbm.at[rows, pl.ds(start, share_width)]
        copies.append(pltpu.make_async_copy(columns, rows_ref.at[rows], semaphores.at[chunk]))
        copies[-1].start()
    degrees_copy.wait()
    roots = lax.rsqrt(degrees_ref[...].astype(jnp.float32))
    for chunk in range(chunks):
        copies[chunk].wait()
        for at in range(chunk * chunk_rows, (chunk + 1) * chunk_rows, 128):
            row = at // 128
            by_row = jnp.broadcast_to(roots[row : row + 1, :], (128, 128)).T
            for column in range(0, share_width, 128):
                part = rows_ref[at : at + 128, column : column + 128].astype(jnp.float32) * by_row
                scaled_ref[at : at + 128, column : column + 128] = part.astype(scaled_ref.dtype)


def payload_kernel(plan, facts_ref, words_ref, features_ref, roots_ref, pairs_ref, turned_ref):
    word_rows = plan.slots * 16
    for step in range(2 * plan.pairs):
        start = ((step % 2) * plan.pairs + step // 2) * plan.pair_rows
        words = words_ref[step].astype(jnp.float32).astype(pairs_ref.dtype)
        pairs_ref[start : start + word_rows, :] = words
        facts = jnp.broadcast_to(facts_ref[step : step + 1, :].astype(jnp.float32), (16, 128))
        pairs_ref[start + word_rows : start + plan.pair_rows, :] = facts.astype(pairs_ref.dtype)
    for at in range(0, features_ref.shape[0], 128):
        part = features_ref[at : at + 128, :].astype(jnp.float32).T * roots_ref[:, at : at + 128]
        turned_ref[:, at : at + 128] = part.astype(turned_ref.dtype)


SMEM = pl.BlockSpec(memory_space=pltpu.SMEM)
VMEM = pl.BlockSpec(memory_space=pltpu.VMEM)
COST = pl.CostEstimate(flops=1, bytes_accessed=1, transcendentals=0)
PARAMS = pltpu.CompilerParams(vmem_limit_bytes=12 * 1024 * 1024)


def in_hbm(block):
    return pltpu.with_memory_space_constraint(block, pltpu.HBM)


def per_device(features, out_grad, weight, block_words, block_coords, block_counts, degrees):
    slab_rows, width = out_grad.shape
    rep_size = lax.axis_size("rep")
    blk_size = lax.axis_size("blk")
    chips = blk_size // CORES
    rows_of_chips = chips // COLUMNS
    rep_index = lax.axis_index("rep")
    blk_index = lax.axis_index("blk")
    core = blk_index % CORES
    chip = blk_index // CORES
    share_width = width // rep_size
    share_rows = slab_rows // rep_size
    slot_total = block_words.shape[2]
    half_steps = block_words.shape[1] // 2

    inverse_root = lax.rsqrt(degrees.astype(jnp.float32))
    if share_width % 128 == 0 and slab_rows % 1024 == 0:
        scaled = pl.pallas_call(
            functools.partial(scale_kernel, share_width),
            out_shape=pltpu.VMEM((slab_rows, share_width), jnp.bfloat16),
            in_specs=[pl.BlockSpec(memory_space=pltpu.HBM)] * 2,
            out_specs=VMEM,
            scratch_shapes=[
                pltpu.VMEM((slab_rows // 128, 128), jnp.int32),
                pltpu.VMEM((slab_rows, share_width), jnp.bfloat16),
                pltpu.SemaphoreType.DMA((3,)),
            ],
            compiler_params=PARAMS,
            name="scale",
        )(in_hbm(degrees.reshape(slab_rows // 128, 128)), in_hbm(out_grad))
    else:
        own_columns = lax.dynamic_slice_in_dim(out_grad, rep_index * share_width, share_width, 1)
        scaled = (own_columns.astype(jnp.float32) * inverse_root[:, None]).astype(jnp.bfloat16)

    forward, backward = along_ring(scaled, 1), along_ring(scaled, -1)

    block_words, features, _ = lax.optimization_barrier((block_words, features, scaled))
    plan = Plan(rep_size, slot_total, half_steps)
    facts = jnp.concatenate(
        [block_counts[0][:, None], block_coords[0].reshape(2 * half_steps, 2 * slot_total)], axis=1
    )
    facts = jnp.pad(facts, ((0, 0), (0, 128 - plan.facts)))
    words_rows = half_steps * plan.pair_rows
    share_root = lax.dynamic_slice_in_dim(inverse_root, rep_index * share_rows, share_rows, 0)
    pairs, turned = pl.pallas_call(
        functools.partial(payload_kernel, plan),
        out_shape=(
            jax.ShapeDtypeStruct((2 * words_rows, 128), jnp.bfloat16),
            jax.ShapeDtypeStruct((width, share_rows), jnp.bfloat16),
        ),
        in_specs=[VMEM] * 4,
        out_specs=(VMEM, VMEM),
        compiler_params=PARAMS,
        cost_estimate=COST,
        name="payload",
    )(facts, block_words[0].reshape(2 * half_steps, slot_total * 16, 128), features, share_root[None])
    both_pieces = from_all_reps(pairs)
    other_pieces = [across_cores(piece[words_rows:]) for piece in both_pieces]
    own_pieces = [piece[:words_rows] for piece in both_pieces]
    own_features = from_all_reps(turned)
    other_features = [across_cores(piece) for piece in own_features]

    def facts_of(piece):
        rows = piece[:words_rows].reshape(half_steps, plan.pair_rows, 128)[:, slot_total * 16]
        return rows[:, : plan.facts].astype(jnp.int32).reshape(-1)

    ring_row = chip // COLUMNS
    place = jnp.where(chip % COLUMNS == 0, ring_row, chips - 1 - ring_row)
    distances = [0]
    for step in range(1, chips // 2):
        distances += [-step, step]
    distances.append(chips // 2)
    entries = []
    for distance in distances:
        at = (place + distance) % chips
        source = jnp.where(at < rows_of_chips, at * COLUMNS, (chips - 1 - at) * COLUMNS + 1)
        for target in range(2):
            offset = (source - chip - jnp.where(core == 0, target, 0)) % chips
            entries += [(rep_index - offset // half_steps) % rep_size, offset % half_steps]
    entries += [(rep_index - d) % rep_size for d in range(rep_size)]
    table = [facts_of(piece) for pair in zip(own_pieces, other_pieces) for piece in pair]
    table = jnp.concatenate(table + [jnp.stack(entries).astype(jnp.int32)])

    slabs = [scaled]
    for step in range(1, chips // 2):
        slabs += [forward, backward]
        forward, backward = along_ring(forward, 1), along_ring(backward, -1)
    del backward

    slab_shape = jax.ShapeDtypeStruct((slab_rows, share_width), jnp.float32)
    sent_shape = jax.ShapeDtypeStruct((slab_rows, share_width), jnp.bfloat16)
    term_shape = jax.ShapeDtypeStruct((width, share_width), jnp.bfloat16)

    def add_slabs(first_slab, slabs, sums):
        operands = own_pieces + other_pieces + slabs
        aliases = {1 + len(operands) + target: target for target in range(len(sums))}
        operands = operands + sums
        return pl.pallas_call(
            functools.partial(adding_kernel, plan, first_slab, len(slabs)),
            out_shape=(slab_shape, slab_shape),
            in_specs=[SMEM] + [VMEM] * len(operands),
            out_specs=(VMEM, VMEM),
            input_output_aliases=aliases,
            compiler_params=PARAMS,
            cost_estimate=COST,
            name="add_slabs",
        )(table, *operands)

    early = len(slabs) - 4
    sums = add_slabs(0, slabs[:early], [])
    sums = add_slabs(early, slabs[early:-1], list(sums))
    sums = add_slabs(len(slabs) - 1, slabs[-1:], list(sums))
    own_sums, other_sums, term = pl.pallas_call(
        functools.partial(last_kernel, plan, len(slabs)),
        out_shape=(slab_shape, sent_shape, term_shape),
        in_specs=[SMEM] + [VMEM] * (4 * rep_size + 3),
        out_specs=(VMEM,) * 3,
        scratch_shapes=[pltpu.VMEM((slab_rows, share_width), jnp.float32)],
        compiler_params=PARAMS,
        cost_estimate=COST,
        name="last_slab",
    )(table, *own_pieces, *other_pieces, *own_features, *other_features, forward, *sums)

    def wide(values):
        return values.astype(jnp.float32)

    total = (wide(term) + wide(across_cores(term))).astype(jnp.bfloat16)
    own_sums = own_sums + wide(across_cores(other_sums))
    aggregated = (own_sums * inverse_root[:, None]).astype(jnp.bfloat16)
    row_bits = [1 << bit for bit in range(rows_of_chips.bit_length() - 1)]
    one = across(total, (row_bits[0] | row_bits[1], 0, 0), (row_bits[1], 0, 0))
    two = across(total, None, (row_bits[0], 0, 0))
    part = wide(one) + wide(jnp.where(core == 0, total, two))
    part, aggregated = lax.optimization_barrier((part, aggregated))
    total = part + across_cores(part)
    for bit in row_bits[2:]:
        total = total.astype(jnp.bfloat16)
        total = wide(total) + wide(across(total, (bit, 0, 0), (bit, 0, 0)))
    total = total.astype(jnp.bfloat16)
    result = jnp.zeros((share_rows, width), jnp.float32)
    shares = []
    for d in range(rep_size):
        rows_to = ((rep_index + d) % rep_size) * share_rows
        part = lax.dynamic_slice_in_dim(aggregated, rows_to, share_rows, 0)
        if d:
            far = across(total, (0, 1, 0), (0, 1, d))
            part, near = along_rep(part, d), along_rep(total, d)
            shares.append(wide(jnp.where(core == 0, total, near)) + wide(far))
        columns_at = ((rep_index - d) % rep_size) * share_width
        side = lax.dynamic_slice_in_dim(weight, columns_at, share_width, 1)
        result = result + lax.dot_general(
            part, side, (((1,), (1,)), ((), ())), preferred_element_type=jnp.float32
        )
    input_grad = result.astype(jnp.bfloat16)
    shares = jnp.stack(shares).astype(jnp.bfloat16)
    shares, input_grad = lax.optimization_barrier((shares, input_grad))
    others = across_cores(shares)
    own_share = jnp.where(core == 0, shares[0], others[0])
    other_shares = jnp.where(core == 0, others, shares)
    weight_grad = jnp.zeros((width, width), jnp.float32)
    for d in range(rep_size):
        columns_at = ((rep_index - d) % rep_size) * share_width
        share = other_shares[d - 1] if d else own_share
        weight_grad = lax.dynamic_update_slice_in_dim(weight_grad, wide(share), columns_at, 1)
    weight_grad = weight_grad * (1.0 / math.sqrt(slab_rows * blk_size))
    return (input_grad, weight_grad)


def solution(mesh):
    return jax.shard_map(
        per_device,
        mesh=mesh,
        in_specs=(
            P(("blk", "rep"), None),
            P("blk", None),
            P(),
            P("blk", "rep", None, None, None),
            P("blk", "rep", None, None),
            P("blk", "rep"),
            P("blk"),
        ),
        out_specs=(P(("blk", "rep"), None), P()),
        check_vma=False,
    )
```
